256 devices in a mesh: lat: 8 (over x, y_hi), lon: 32 (over z, y_lo, core).
Axes of the slice: x: 4, y: 4 (y_hi: 2, y_lo: 2; y = y_hi * 2 + y_lo), z: 8, core: 2. Of those that a mesh axis runs over, the one named last changes fastest.
Arguments:
- coarse: bfloat16 [40, 48, 320], P(None, 'lat', 'lon'), may hold values from -6 to 6
- row_map: int32 [384], replicated, may hold values from 0 to 46, as said below
- row_frac: float32 [384], replicated, may hold values from 0 to 1
- col_map: int32 [2560], replicated, may hold values from 0 to 319, as said below
- col_frac: float32 [2560], replicated, may hold values from 0 to 1
- noise_init: float32 [4, 384, 2560], P(None, 'lat', 'lon'), may hold values from -6 to 6
- noise_churn: float32 [4, 384, 2560], P(None, 'lat', 'lon'), may hold values from -6 to 6
- w_state: bfloat16 [128, 36], replicated, may hold values from -1 to 1
- w_cond: bfloat16 [128, 40], replicated, may hold values from -1 to 1
- w_expand: bfloat16 [128, 128], replicated, may hold values from -0.5 to 0.5
- w_project: bfloat16 [128, 128], replicated, may hold values from -0.5 to 0.5
- w_levels: bfloat16 [4, 9, 128, 128], replicated, may hold values from -0.1875 to 0.1875
- w_final: bfloat16 [9, 4, 128], replicated, may hold values from -0.1875 to 0.1875
Outputs:
- final_state: float32 [4, 384, 2560], P(None, 'lat', 'lon')
The draws below stay inside these ranges and needn't reach their ends.
Inputs may be any that keep to these rules, and one draw needn't show every extreme that they name: |row_map[y] - y // 8| <= 2 for every fine row y, and both +2 and -2 occur. col_map[x] - x // 8, taken modulo 320 into -2 to 2, lies within that range for every fine column x, and both ends occur.
All inputs are finite; a program needn't handle non-finite values.
Results may differ from the reference program's by a relative error of at most 0.014.
Values may be sent and summed in bfloat16 or wider, within the bound.
No kernel may reach another device: no remote copies, remote signals or barrier semaphores. Data moves between devices by JAX's collectives and lax.ppermute only.
A program may use at most 128 MiB of HBM per device.

```python
import math
import jax
import jax.numpy as jnp
from jax import lax

CHANNELS_IN = 40
CHANNELS_OUT = 4
WIDTH = 128
LEVELS = 4
RATIO = 8
MARGIN = 24
MAP_DRIFT = 2
TILE_ROWS = 48
TILE_COLS = 80
GRID_ROWS = 384
GRID_COLS = 2560
COARSE_ROWS = 48
COARSE_COLS = 320
N_LAT = 8
N_LON = 32


def draw_row_map(key, part):
    key = jax.random.fold_in(key, 7)
    key_drift, key_place = jax.random.split(key)
    positions = jnp.arange(GRID_ROWS, dtype=jnp.int32)
    drift_rows = jax.random.randint(key_drift, (GRID_ROWS,), -MAP_DRIFT, MAP_DRIFT + 1, dtype=jnp.int32)
    marked = jax.random.randint(key_place, (), GRID_ROWS // 4, 3 * GRID_ROWS // 4, dtype=jnp.int32)
    drift_rows = jnp.where(positions == marked, MAP_DRIFT, drift_rows)
    drift_rows = jnp.where(positions == marked - GRID_ROWS // 8, -MAP_DRIFT, drift_rows)
    mapped = jnp.clip(positions // RATIO + drift_rows, 0, COARSE_ROWS - 2)
    mapped = jnp.where(positions == 0, 0, mapped)
    mapped = jnp.where(positions == GRID_ROWS - 1, COARSE_ROWS - 2, mapped)
    return mapped.astype(jnp.int32)


def draw_col_map(key, part):
    key = jax.random.fold_in(key, 13)
    key_drift, key_place = jax.random.split(key)
    positions = jnp.arange(GRID_COLS, dtype=jnp.int32)
    drift_cols = jax.random.randint(key_drift, (GRID_COLS,), -MAP_DRIFT, MAP_DRIFT + 1, dtype=jnp.int32)
    marked = jax.random.randint(key_place, (), GRID_COLS // 4, 3 * GRID_COLS // 4, dtype=jnp.int32)
    drift_cols = jnp.where(positions == marked, MAP_DRIFT, drift_cols)
    drift_cols = jnp.where(positions == marked - GRID_COLS // 8, -MAP_DRIFT, drift_cols)
    drift_cols = jnp.where(positions == 0, 0, drift_cols)
    drift_cols = jnp.where(positions == 1, -1, drift_cols)
    mapped = jnp.mod(positions // RATIO + drift_cols, COARSE_COLS)
    return mapped.astype(jnp.int32)


def shard_levels(own_key, extent, cuts, least, top_value):
    level, own = 1.0, jax.random.fold_in(own_key, 6)
    for axis_at, shards_of in cuts:
        heights = jnp.exp(jax.random.uniform(jax.random.fold_in(own, axis_at), (shards_of,), jnp.float32, least / len(cuts), top_value / len(cuts)))
        level = level * jnp.repeat(heights, extent[axis_at] // shards_of).reshape([-1 if axis == axis_at else 1 for axis in range(len(extent))])
    return level


def gaussian(rng, extent, spread, limit, shards=(), kind=jnp.bfloat16):
    result = spread * jax.random.normal(rng, extent, jnp.float32)
    if shards:
        result = result * shard_levels(rng, extent, shards, -0.22, 0.18)
    return jnp.clip(result, -limit, limit).astype(kind)


def setup_inputs(seed: int = 0) -> dict:
    splits = jax.random.split(jax.random.key(seed), 14)
    coarse = gaussian(splits[0], (CHANNELS_IN, COARSE_ROWS, COARSE_COLS), 1.0, 6.0, ((1, 8), (2, 32)))
    row_map = draw_row_map(jax.random.fold_in(splits[13], 71), 0)
    row_frac = jnp.clip(jax.random.uniform(splits[2], (GRID_ROWS,), jnp.float32, 0.0, 1.0), 0.0, 1.0)
    col_map = draw_col_map(jax.random.fold_in(splits[13], 71), 0)
    col_frac = jnp.clip(jax.random.uniform(splits[4], (GRID_COLS,), jnp.float32, 0.0, 1.0), 0.0, 1.0)
    noise_init = gaussian(splits[5], (CHANNELS_OUT, GRID_ROWS, GRID_COLS), 1.0, 6.0, ((1, 8), (2, 32)), jnp.float32)
    noise_churn = gaussian(splits[6], (CHANNELS_OUT, GRID_ROWS, GRID_COLS), 1.0, 6.0, ((1, 8), (2, 32)), jnp.float32)
    w_state = gaussian(splits[7], (WIDTH, 9 * CHANNELS_OUT), (9 * CHANNELS_OUT) ** -0.5, 1.0)
    w_cond = gaussian(splits[8], (WIDTH, CHANNELS_IN), CHANNELS_IN ** -0.5, 1.0)
    w_expand = gaussian(splits[9], (WIDTH, WIDTH), WIDTH ** -0.5, 0.5)
    w_project = gaussian(splits[10], (WIDTH, WIDTH), WIDTH ** -0.5, 0.5)
    w_levels = gaussian(splits[11], (LEVELS, 9, WIDTH, WIDTH), (9 * WIDTH) ** -0.5, 0.1875)
    w_final = gaussian(splits[12], (9, CHANNELS_OUT, WIDTH), (9 * WIDTH) ** -0.5, 0.1875)
    return dict(coarse=coarse, row_map=row_map, row_frac=row_frac, col_map=col_map, col_frac=col_frac, noise_init=noise_init, noise_churn=noise_churn, w_state=w_state, w_cond=w_cond, w_expand=w_expand, w_project=w_project, w_levels=w_levels, w_final=w_final)


sigma_data = 0.5
level_first = 4.0
level_second = 1.0
level_raised = 1.5
level_final = 0.25
epsilon = 1e-06

def rounded(value):
    return lax.optimization_barrier(value.astype(jnp.bfloat16)).astype(jnp.float32)

def upsample(coarse, row_map, row_frac, col_map, col_frac):
    coarse_f32 = coarse.astype(jnp.float32)
    upper = jnp.take(coarse_f32, row_map, axis=1)
    lower = jnp.take(coarse_f32, row_map + 1, axis=1)
    rows_done = (1.0 - row_frac)[None, :, None] * upper + row_frac[None, :, None] * lower
    left_cols = jnp.take(rows_done, col_map, axis=2)
    right_cols = jnp.take(rows_done, jnp.mod(col_map + 1, COARSE_COLS), axis=2)
    fine_field = (1.0 - col_frac)[None, None, :] * left_cols + col_frac[None, None, :] * right_cols
    return fine_field.astype(jnp.bfloat16)

def shifted_taps(field):
    height = field.shape[1]
    breadth = field.shape[2]
    padded = jnp.pad(field, ((0, 0), (1, 1), (1, 1)))
    return jnp.stack([padded[:, row_step:row_step + height, col_step:col_step + breadth] for row_step in range(3) for col_step in range(3)], axis=0)

def channel_norm(values):
    return values * lax.rsqrt(lax.optimization_barrier(jnp.mean(values * values, axis=0, keepdims=True)) + epsilon)

def halve_grid(field):
    channels, height, breadth = field.shape
    return lax.optimization_barrier(jnp.mean(field.reshape(channels, height // 2, 2, breadth // 2, 2), axis=(2, 4), dtype=jnp.float32))

def enlarge(field):
    return jnp.repeat(jnp.repeat(field, 2, axis=1), 2, axis=2)

def denoise(state_patch, cond_patch, noise_level, w_state, w_cond, w_expand, w_project, w_levels, w_final):
    total_sq = noise_level * noise_level + sigma_data * sigma_data
    scaled = rounded(state_patch * (1.0 / math.sqrt(total_sq)))
    height = scaled.shape[1]
    breadth = scaled.shape[2]
    tap_stack = shifted_taps(scaled).reshape(9 * CHANNELS_OUT, height, breadth)
    pre_norm = jnp.einsum('wk,kpq->wpq', w_state.astype(jnp.float32), tap_stack)
    pre_norm = pre_norm + jnp.einsum('wc,cpq->wpq', w_cond.astype(jnp.float32), cond_patch.astype(jnp.float32))
    hidden = rounded(jax.nn.silu(channel_norm(pre_norm)))
    level_acts = [hidden]
    current = hidden
    for level_index in range(LEVELS):
        pooled = rounded(halve_grid(current))
        level_taps = shifted_taps(pooled)
        conv_out = jnp.einsum('koi,kipq->opq', w_levels[level_index].astype(jnp.float32), level_taps)
        current = rounded(jax.nn.silu(channel_norm(conv_out)))
        level_acts.append(current)
    merged = level_acts[LEVELS]
    for level_index in range(LEVELS - 1, 0, -1):
        merged = level_acts[level_index] + enlarge(merged)
    joined = rounded(hidden + enlarge(merged))
    inner_act = rounded(jax.nn.silu(jnp.einsum('vw,wpq->vpq', w_expand.astype(jnp.float32), joined)))
    mixed_act = rounded(joined + jnp.einsum('vw,wpq->vpq', w_project.astype(jnp.float32), inner_act))
    per_tap = jnp.einsum('koi,ipq->kopq', w_final.astype(jnp.float32), mixed_act)
    padded_taps = jnp.pad(per_tap, ((0, 0), (0, 0), (1, 1), (1, 1)))
    refined = sum((padded_taps[row_step * 3 + col_step, :, row_step:row_step + height, col_step:col_step + breadth] for row_step in range(3) for col_step in range(3)))
    skip_scale = sigma_data * sigma_data / total_sq
    out_scale = noise_level * sigma_data / math.sqrt(total_sq)
    return skip_scale * state_patch + out_scale * refined

def pad_field(field):
    wrapped = jnp.concatenate([field[:, :, GRID_COLS - MARGIN:], field, field[:, :, :MARGIN]], axis=2)
    return jnp.pad(wrapped, ((0, 0), (MARGIN, MARGIN), (0, 0)))

def cover_count():
    rows_all = jnp.arange(GRID_ROWS, dtype=jnp.int32)
    row_starts = jnp.arange(N_LAT, dtype=jnp.int32) * TILE_ROWS - MARGIN
    lat_cover = lax.optimization_barrier(jnp.sum(((rows_all[None, :] >= row_starts[:, None]) & (rows_all[None, :] < row_starts[:, None] + TILE_ROWS + 2 * MARGIN)).astype(jnp.float32), axis=0))
    cols_all = jnp.arange(GRID_COLS, dtype=jnp.int32)
    col_starts = jnp.arange(N_LON, dtype=jnp.int32) * TILE_COLS - MARGIN
    lon_cover = lax.optimization_barrier(jnp.sum((jnp.mod(cols_all[None, :] - col_starts[:, None], GRID_COLS) < TILE_COLS + 2 * MARGIN).astype(jnp.float32), axis=0))
    return lat_cover[:, None] * lon_cover[None, :]

def blend(state, cond_padded, noise_level, weights):
    state_padded = pad_field(state)
    patch_rows = TILE_ROWS + 2 * MARGIN
    patch_cols = TILE_COLS + 2 * MARGIN
    zero_index = jnp.zeros((), jnp.int32)

    def visit(total, index):
        row_start = (index // N_LON * TILE_ROWS).astype(jnp.int32)
        col_start = (jnp.mod(index, N_LON) * TILE_COLS).astype(jnp.int32)
        state_patch = lax.dynamic_slice(state_padded, (zero_index, row_start, col_start), (CHANNELS_OUT, patch_rows, patch_cols))
        cond_patch = lax.dynamic_slice(cond_padded, (zero_index, row_start, col_start), (CHANNELS_IN, patch_rows, patch_cols))
        denoised = denoise(state_patch, cond_patch, noise_level, *weights)
        current = lax.dynamic_slice(total, (zero_index, row_start, col_start), (CHANNELS_OUT, patch_rows, patch_cols))
        return (lax.dynamic_update_slice(total, current + denoised, (zero_index, row_start, col_start)), None)
    empty = jnp.zeros((CHANNELS_OUT, GRID_ROWS + 2 * MARGIN, GRID_COLS + 2 * MARGIN), jnp.float32)
    total, _ = lax.scan(visit, empty, jnp.arange(N_LAT * N_LON, dtype=jnp.int32))
    middle = total[:, MARGIN:MARGIN + GRID_ROWS, :]
    core = middle[:, :, MARGIN:MARGIN + GRID_COLS]
    core = core.at[:, :, GRID_COLS - MARGIN:].add(middle[:, :, :MARGIN])
    core = core.at[:, :, :MARGIN].add(middle[:, :, MARGIN + GRID_COLS:])
    return core / cover_count()[None]

def reference(coarse, row_map, row_frac, col_map, col_frac, noise_init, noise_churn, w_state, w_cond, w_expand, w_project, w_levels, w_final):
    weights = (w_state, w_cond, w_expand, w_project, w_levels, w_final)
    cond_padded = pad_field(upsample(coarse, row_map, row_frac, col_map, col_frac))
    state = level_first * noise_init
    blended = blend(state, cond_padded, level_first, weights)
    state = state + (level_second - level_first) * (state - blended) / level_first
    state = state + math.sqrt(level_raised * level_raised - level_second * level_second) * noise_churn
    blended = blend(state, cond_padded, level_raised, weights)
    return state + (level_final - level_raised) * (state - blended) / level_raised
```

```python
import math

import jax
import jax.numpy as jnp
import numpy as np
from jax import lax
from jax.experimental import pallas as pl
from jax.experimental.pallas import tpu as pltpu
from jax.sharding import PartitionSpec as P

MARGIN = 24
TILE_ROWS, TILE_COLS = 48, 80
PATCH_ROWS, PATCH_COLS = 96, 128
CH = 128
ROWS = 4 * PATCH_ROWS
PAIRS = PATCH_ROWS // 2
SIDE = 16
COARSE_SLOTS = 48

sigma_data = 0.5
level_first = 4.0
level_second = 1.0
level_raised = 1.5
level_final = 0.25
epsilon = 1e-06

F32 = jnp.float32
BF16 = jnp.bfloat16


def _constants():
    place = np.arange(128)
    column = 8 * (place % 16) + place // 16
    perm = (column[:, None] == np.arange(128)[None, :]).astype(np.float32)
    back = []
    for shift in range(3):
        one = (column[:, None] == (np.arange(128) + shift - 1)[None, :]).astype(np.float32)
        back += [one, one]
    back = np.concatenate(back, 0)
    pick_in = np.zeros((2, 48, 36), np.float32)
    pick_out = np.zeros((2, 48, 36), np.float32)
    for pi in range(2):
        for dc in range(3):
            for pp in range(4):
                for e in range(4):
                    dr = pp - pi
                    if 0 <= dr <= 2:
                        pick_in[pi, dc * 16 + pp * 4 + e, (3 * dr + dc) * 4 + e] = 1.0
                    dr = pi + 2 - pp
                    if 0 <= dr <= 2:
                        pick_out[pi, dc * 16 + pp * 4 + e, (3 * dr + dc) * 4 + e] = 1.0
    pool = np.zeros((9, 6, 8, 12, 16), np.float32)
    for dr in range(3):
        for dc in range(3):
            for r in range(6):
                for c in range(8):
                    rr, cc = r + dr - 1, c + dc - 1
                    if 0 <= rr < 6 and 0 <= cc < 8:
                        pool[3 * dr + dc, r, c, 2 * rr : 2 * rr + 2, 2 * cc : 2 * cc + 2] = 0.25
    pool = pool.reshape(432, 192)
    grow = np.zeros((12, 16, 6, 8), np.float32)
    for r in range(12):
        for c in range(16):
            grow[r, c, r // 2, c // 2] = 1.0
    grow = grow.reshape(192, 48)
    return perm, back, pick_in, pick_out, pool, grow


PERM, BACK, PICK_IN, PICK_OUT, POOL, GROW = _constants()


def dot_nt(a, b):
    return lax.dot_general(a, b, (((1,), (1,)), ((), ())), preferred_element_type=F32)


def dot_nn(a, b):
    return jnp.dot(a, b, preferred_element_type=F32)


def lanes(shape):
    return lax.broadcasted_iota(jnp.int32, shape, 1)


def roll_lanes(value, amount):
    amount = amount % 128
    return value if amount == 0 else pltpu.roll(value, amount, 1)


def prepare_kernel(
    w_state, w_expand, w_project, w_levels, w_final, eye, pick_in, pick_out,
    first_w, expand_w, project_w, level_w, final_w, flat_final,
):
    unit = eye[...]
    for k in range(9):
        flat_final[4 * k : 4 * k + 4, :] = w_final[k].astype(F32)
    final_rows = flat_final[...].astype(BF16)
    state_rows = w_state[...]
    for pi in range(2):
        part = slice(pi * 128, pi * 128 + 128)
        first_w[:, part] = dot_nn(pick_in[pi], state_rows).astype(BF16)
        final_w[:, part] = dot_nn(pick_out[pi], final_rows).astype(BF16)
    zero = jnp.zeros((128, 128), BF16)
    for source, target, factor in ((w_expand, expand_w, 0.5), (w_project, project_w, 1.0)):
        block = (dot_nt(unit, source[...]) * factor).astype(BF16)
        target[0:128, 0:128] = block
        target[128:256, 128:256] = block
        target[0:128, 128:256] = zero
        target[128:256, 0:128] = zero
    for level in range(4):
        for k in range(9):
            level_w[level, k * 128 : k * 128 + 128, :] = dot_nt(unit, w_levels[level, k]).astype(BF16)


def pack_rows_kernel(noise_init, noise_churn, coarse, to_upper, to_lower, own, own_coarse, padded):
    for which, noise in enumerate((noise_init, noise_churn)):
        for e in range(4):
            padded[which, pl.ds(e, TILE_ROWS, stride=4), 0:TILE_COLS] = noise[e]
    own_coarse[...] = jnp.zeros((96, 128), F32)
    for k in range(10):
        own_coarse[pl.ds(k, 6, stride=16), 0:40] = coarse[k].astype(F32)
    lane = lanes((96, 128))
    placed = roll_lanes(own_coarse[...], 80)
    for which in range(2):
        own[which] = padded[which]
        for target, start in ((to_upper, 0), (to_lower, 96)):
            part = padded[which, start : start + 96, :]
            if which == 0:
                part = jnp.where(lane < 80, part, placed)
            target[which * 96 : which * 96 + 96, :] = part.astype(BF16)


def pack_cols_kernel(from_upper, from_lower, own, own_coarse, to_left, to_right, strip, coarse_strip):
    lane = lanes((192, 128))
    for which in range(2):
        rows = slice(which * 96, which * 96 + 96)
        strip[which, 0:96, :] = roll_lanes(from_upper[rows, :].astype(F32), MARGIN)
        strip[which, 96:288, :] = roll_lanes(own[which], MARGIN)
        strip[which, 288:384, :] = roll_lanes(from_lower[rows, :].astype(F32), MARGIN)
    left = right = None
    for group in range(4):
        part = strip[group // 2, (group % 2) * 192 : (group % 2) * 192 + 192, :]
        for_left = roll_lanes(part, 32 * group - 24)
        for_right = roll_lanes(part, 32 * group - 80)
        inside = (lane >= 32 * group) & (lane < 32 * group + 32)
        left = for_left if group == 0 else jnp.where(inside, for_left, left)
        right = for_right if group == 0 else jnp.where(inside, for_right, right)
    to_left[0:192, :] = left.astype(BF16)
    to_right[0:192, :] = right.astype(BF16)
    narrow = lanes((96, 128))
    above = roll_lanes(from_upper[0:96, :].astype(F32), -80)
    middle = own_coarse[...]
    below = roll_lanes(from_lower[0:96, :].astype(F32), -80)
    for index, part in enumerate((above, middle, below)):
        coarse_strip[index * 96 : index * 96 + 96, :] = jnp.where(narrow < 40, part, 0.0)
    packed = jnp.where(narrow < 40, above, jnp.where(narrow < 80, roll_lanes(middle, 40), roll_lanes(below, 80)))
    to_left[192:288, :] = packed.astype(BF16)
    to_right[192:288, :] = packed.astype(BF16)


def pad_store(target, row, pooled, groups):
    rows = pooled.shape[0]
    place = lax.broadcasted_iota(jnp.int32, (SIDE, 128), 0)
    target[pl.ds(row + 1, rows), SIDE : SIDE + groups * SIDE, :] = pooled.reshape(
        rows, groups * SIDE, 128
    ).astype(BF16)
    for r in range(rows):
        before = pltpu.roll(pooled[r, groups - 1], 1, 0)
        after = pltpu.roll(pooled[r, 0], SIDE - 1, 0)
        target[row + 1 + r, 0:SIDE, :] = jnp.where(place == 0, 0.0, before).astype(BF16)
        target[row + 1 + r, SIDE + groups * SIDE : 2 * SIDE + groups * SIDE, :] = jnp.where(
            place == SIDE - 1, 0.0, after
        ).astype(BF16)


def halve(values, rows, groups):
    grouped = values.reshape(rows // 2, 2, groups // 2, 2, SIDE, 128)
    return 0.25 * (
        (grouped[:, 0, :, 0] + grouped[:, 0, :, 1]) + (grouped[:, 1, :, 0] + grouped[:, 1, :, 1])
    )


def norm_silu(values, mean_w):
    squares = dot_nn((values * values).astype(BF16), mean_w)
    half = values * lax.rsqrt(squares + 4.0 * epsilon)
    return half + half * jnp.tanh(half)


def conv_rows(source, weight, row, rows, groups):
    taps = [
        source[pl.ds(row + dr, rows), dc * SIDE : dc * SIDE + groups * SIDE, :].reshape(
            rows * groups * SIDE, 128
        )
        for dr in range(3)
        for dc in range(3)
    ]
    return dot_nn(jnp.concatenate(taps, axis=1), weight)


CORE_SCRATCH = [
    pltpu.VMEM((3, 400, 128), F32),
    pltpu.VMEM((PAIRS, 128, 256), BF16),
    pltpu.VMEM((50, 96, 128), BF16),
    pltpu.VMEM((26, 64, 128), BF16),
    pltpu.VMEM((14, 48, 128), BF16),
    pltpu.VMEM((48, 64, 128), F32),
    pltpu.VMEM((24, 32, 128), F32),
    pltpu.VMEM((3, 392, 128), F32),
    pltpu.VMEM((3, 400, 128), F32),
]


def denoise(
    state, colmix, coarse_fields, lat, row_map, row_frac, weights, constants, scratch, noise_level, out
):
    first_w, expand_w, project_w, level_w, final_w = weights
    perm, back, mean_w, pool, grow = constants
    scaled, hidden, pooled1, pooled2, pooled3, level1, level2, taps_a, taps_b = scratch
    total_sq = noise_level * noise_level + sigma_data * sigma_data

    for shift in range(3):
        scaled[shift, 0:8, :] = jnp.zeros((8, 128), F32)
        scaled[shift, 384:400, :] = jnp.zeros((16, 128), F32)
        taps_a[shift, 384:392, :] = jnp.zeros((8, 128), F32)
        taps_b[shift, 0:8, :] = jnp.zeros((8, 128), F32)
    base = state[...] * (1.0 / math.sqrt(total_sq))
    lane = lanes((ROWS, 128))
    scaled[0, 4 : 4 + ROWS, :] = jnp.where(lane == 0, 0.0, pltpu.roll(base, 1, 1))
    scaled[1, 4 : 4 + ROWS, :] = base
    scaled[2, 4 : 4 + ROWS, :] = jnp.where(lane == 127, 0.0, pltpu.roll(base, 127, 1))
    for buffer, rows in ((pooled1, 50), (pooled2, 26), (pooled3, 14)):
        blank = jnp.zeros(buffer.shape[1:], BF16)
        buffer[0] = blank
        buffer[rows - 1] = blank

    def coarse_row(p):
        y = lat * TILE_ROWS - MARGIN + p
        inside = (y >= 0) & (y < 8 * TILE_ROWS)
        y = jnp.clip(y, 0, 8 * TILE_ROWS - 1)
        at = jnp.clip(row_map[y] - (lat * 6 - 6), 0, 16)
        fraction = row_frac[y]
        near = jnp.where(inside, 1.0 - fraction, 0.0)
        far = jnp.where(inside, fraction, 0.0)
        return near * coarse_fields[at] + far * coarse_fields[at + 1]

    def first(i, carry):
        row = pl.multiple_of(8 * i, 8)
        columns = [scaled[shift, pl.ds(row, 16), :].astype(BF16) for shift in range(3)]
        turned = dot_nt(perm[...], jnp.concatenate(columns + [colmix[...]], axis=0)).astype(BF16)
        fields = jnp.concatenate([coarse_row(2 * i), coarse_row(2 * i + 1)], axis=1).astype(BF16)
        pre = dot_nn(turned, jnp.concatenate([first_w[...], fields], axis=0))
        act = norm_silu(pre, mean_w[...])
        hidden[i] = act.astype(BF16)
        summed = (act[:, 0:128] + act[:, 128:256]).reshape(4, 2, SIDE, 128)
        pad_store(pooled1, i, (0.25 * (summed[:, 0] + summed[:, 1]))[None], 4)
        return carry

    lax.fori_loop(0, PAIRS, first, 0, unroll=2)

    mean_one = mean_w[0:128, 0:128]

    def one(c, carry):
        act = norm_silu(conv_rows(pooled1, level_w[0], 4 * c, 4, 4), mean_one)
        level1[pl.ds(4 * c, 4)] = act.reshape(4, 64, 128)
        pad_store(pooled2, 2 * c, halve(act, 4, 4), 2)
        return carry

    lax.fori_loop(0, 12, one, 0, unroll=2)

    def two(c, carry):
        act = norm_silu(conv_rows(pooled2, level_w[1], 8 * c, 8, 2), mean_one)
        level2[pl.ds(8 * c, 8)] = act.reshape(8, 32, 128)
        pad_store(pooled3, 4 * c, halve(act, 8, 2), 1)
        return carry

    lax.fori_loop(0, 3, two, 0, unroll=True)

    act3 = norm_silu(conv_rows(pooled3, level_w[2], 0, 12, 1), mean_one)
    shifted = dot_nn(pool[...], act3.astype(BF16)).astype(BF16)
    act4 = norm_silu(
        dot_nn(jnp.concatenate([shifted[48 * k : 48 * k + 48] for k in range(9)], axis=1), level_w[3]),
        mean_one,
    )
    merged3 = act3 + dot_nn(grow[...], act4.astype(BF16))
    merged2 = level2[...].reshape(12, 2, 2, SIDE, 128) + merged3.reshape(12, 1, 1, SIDE, 128)
    level2[...] = merged2.reshape(24, 32, 128)

    def last(i, carry):
        coarse2 = level2[i // 2].reshape(2, 1, SIDE, 128)
        merged1 = level1[i].reshape(2, 2, SIDE, 128) + coarse2
        merged1 = merged1.reshape(4, 1, SIDE, 128)
        merged1 = jnp.concatenate([merged1, merged1], axis=1).reshape(128, 128)
        joined = (hidden[i].astype(F32) + jnp.concatenate([merged1, merged1], axis=1)).astype(BF16)
        half = dot_nn(joined, expand_w[...])
        inner = (half + half * jnp.tanh(half)).astype(BF16)
        mixed = (joined.astype(F32) + dot_nn(inner, project_w[...])).astype(BF16)
        taps = dot_nt(final_w[...], mixed)
        row = pl.multiple_of(8 * i, 8)
        for shift in range(3):
            taps_a[shift, pl.ds(row, 8), :] = taps[16 * shift : 16 * shift + 8]
            taps_b[shift, pl.ds(row + 8, 8), :] = taps[16 * shift + 8 : 16 * shift + 16]
        return carry

    lax.fori_loop(0, PAIRS, last, 0, unroll=2)

    parts = []
    for shift in range(3):
        total = taps_a[shift, 4 : 4 + ROWS, :] + taps_b[shift, 4 : 4 + ROWS, :]
        upper = total.astype(BF16)
        parts += [upper, (total - upper.astype(F32)).astype(BF16)]
    refined = dot_nn(jnp.concatenate(parts, axis=1), back[...])
    skip_scale = sigma_data * sigma_data / total_sq
    out_scale = noise_level * sigma_data / math.sqrt(total_sq)
    out[...] = skip_scale * state[...] + out_scale * refined


def inside_rows(lat):
    row = lax.broadcasted_iota(jnp.int32, (ROWS, 128), 0)
    first = jnp.where(lat == 0, 4 * MARGIN, 0)
    last = jnp.where(lat == 7, ROWS - 4 * MARGIN, ROWS)
    return (row >= first) & (row < last)


def first_kernel(
    place, row_map, row_frac, col_map, col_frac, strip, coarse_strip, from_left, from_right, w_cond,
    first_w, expand_w, project_w, level_w, final_w, perm, back, mean_w, pool, grow,
    den, to_upper, to_lower, state, churn, fields, colmix,
    window, *scratch,
):
    lat, lon = place[0], place[1]
    lane = lanes((192, 128))
    inside = inside_rows(lat)
    for which, target in enumerate((state, churn)):
        for part in range(2):
            group = 2 * which + part
            rows = slice(part * 192, part * 192 + 192)
            left = roll_lanes(from_left[0:192, :].astype(F32), -32 * group)
            right = roll_lanes(from_right[0:192, :].astype(F32), 104 - 32 * group)
            target[rows, :] = jnp.where(lane < 24, left, jnp.where(lane < 104, strip[which, rows, :], right))
    state[...] = jnp.where(inside, level_first * state[...], 0.0)

    narrow = lanes((96, 128))
    for t, source in enumerate((from_left, None, from_right)):
        for part in range(3):
            if source is None:
                rows = coarse_strip[part * 96 : part * 96 + 96, :]
            else:
                rows = roll_lanes(source[192:288, :].astype(F32), -40 * part)
            for j in range(6):
                window[part * 6 + j, t * 16 : t * 16 + 16, :] = rows[j * 16 : j * 16 + 16]
    stacked = window[...].reshape(18 * COARSE_SLOTS, 128)[:, 0:40].astype(BF16)
    fields[...] = dot_nn(stacked, w_cond[...]).reshape(18, COARSE_SLOTS, 128)

    offset = col_map[...] - (10 * lon - 10)
    offset = jnp.where(offset < 0, offset + 320, offset)
    offset = jnp.where(offset >= 320, offset - 320, offset)
    slot = lax.broadcasted_iota(jnp.int32, (COARSE_SLOTS, 128), 0)
    tile = jnp.where(slot >= 32, 2, jnp.where(slot >= 16, 1, 0))
    column = jnp.where(slot - 16 * tile < 10, slot - 6 * tile, -1)
    fraction = col_frac[...]
    mix = jnp.where(column == offset, 1.0 - fraction, 0.0) + jnp.where(column == offset + 1, fraction, 0.0)
    colmix[...] = mix.astype(BF16)

    denoise(
        state, colmix, fields, lat, row_map, row_frac,
        (first_w, expand_w, project_w, level_w, final_w), (perm, back, mean_w, pool, grow),
        scratch, level_first, den,
    )
    to_upper[...] = den[0:192, :].astype(BF16)
    to_lower[...] = den[192:384, :].astype(BF16)


def add_rows_kernel(place, den, from_upper, from_lower, total, to_left, to_right):
    lat = place[0]
    has_upper = jnp.where(lat > 0, 1.0, 0.0)
    has_lower = jnp.where(lat < 7, 1.0, 0.0)
    top = den[0:192, :] + has_upper * from_upper[...].astype(F32)
    bottom = den[192:384, :] + has_lower * from_lower[...].astype(F32)
    total[0:192, :] = top
    total[192:384, :] = bottom
    lane = lanes((192, 128))
    to_left[...] = jnp.where(lane < 64, top, roll_lanes(bottom, 64)).astype(BF16)
    to_right[...] = jnp.where(lane < 64, roll_lanes(top, -80), roll_lanes(bottom, 64 - 80)).astype(BF16)


def second_kernel(
    place, row_map, row_frac, total, from_left, from_right, state, churn, fields, colmix,
    first_w, expand_w, project_w, level_w, final_w, perm, back, mean_w, pool, grow,
    den, to_upper, to_lower, raised,
    *scratch,
):
    lat = place[0]
    lane = lanes((192, 128))
    edge = (lane < 48) | (lane >= 80)
    left = from_left[...].astype(F32)
    right = from_right[...].astype(F32)
    inside = inside_rows(lat)
    for part in range(2):
        rows = slice(part * 192, part * 192 + 192)
        from_l = roll_lanes(left, -64 * part)
        from_r = roll_lanes(right, 80 - 64 * part)
        summed = total[rows, :] + jnp.where(lane < 48, from_l, jnp.where(lane >= 80, from_r, 0.0))
        has = (lat > 0) if part == 0 else (lat < 7)
        blended = summed * (jnp.where(has, 0.5, 1.0) * jnp.where(edge, 0.5, 1.0))
        value = state[rows, :]
        value = value + (level_second - level_first) / level_first * (value - blended)
        value = value + math.sqrt(level_raised * level_raised - level_second * level_second) * churn[rows, :]
        raised[rows, :] = value
    raised[...] = jnp.where(inside, raised[...], 0.0)
    denoise(
        raised, colmix, fields, lat, row_map, row_frac,
        (first_w, expand_w, project_w, level_w, final_w), (perm, back, mean_w, pool, grow),
        scratch, level_raised, den,
    )
    to_upper[...] = den[0:96, :].astype(BF16)
    to_lower[...] = den[288:384, :].astype(BF16)


def add_tile_rows_kernel(place, den, from_upper, from_lower, total, to_left, to_right):
    lat = place[0]
    has_upper = jnp.where(lat > 0, 1.0, 0.0)
    has_lower = jnp.where(lat < 7, 1.0, 0.0)
    top = den[96:192, :] + has_upper * from_upper[...].astype(F32)
    bottom = den[192:288, :] + has_lower * from_lower[...].astype(F32)
    total[0:96, :] = top
    total[96:192, :] = bottom
    lane = lanes((96, 128))
    to_left[...] = jnp.where(lane < 64, top, roll_lanes(bottom, 64)).astype(BF16)
    to_right[...] = jnp.where(lane < 64, roll_lanes(top, -104), roll_lanes(bottom, 64 - 104)).astype(BF16)


def finish_kernel(place, total, from_left, from_right, raised, out, rows_ref):
    lat = place[0]
    lane = lanes((96, 128))
    edge = (lane < 48) | (lane >= 80)
    left = from_left[...].astype(F32)
    right = from_right[...].astype(F32)
    for part in range(2):
        rows = slice(part * 96, part * 96 + 96)
        from_l = roll_lanes(left, 24 - 64 * part)
        from_r = roll_lanes(right, 80 - 64 * part)
        use_l = (lane >= 24) & (lane < 48)
        use_r = (lane >= 80) & (lane < 104)
        summed = total[rows, :] + jnp.where(use_l, from_l, jnp.where(use_r, from_r, 0.0))
        has = (lat > 0) if part == 0 else (lat < 7)
        blended = summed * (jnp.where(has, 0.5, 1.0) * jnp.where(edge, 0.5, 1.0))
        value = raised[96 + part * 96 : 192 + part * 96, :]
        value = value + (level_final - level_raised) / level_raised * (value - blended)
        rows_ref[rows, :] = roll_lanes(value, -24)
    for e in range(4):
        out[e] = rows_ref[pl.ds(e, TILE_ROWS, stride=4), 0:TILE_COLS]


def shape(dims, dtype):
    return jax.ShapeDtypeStruct(dims, dtype)


def call(kernel, operands, outs, scratch=(), scalars=0, cost=(0, 0, 0)):
    smem = pl.BlockSpec(memory_space=pltpu.SMEM)
    vmem = pl.BlockSpec(memory_space=pltpu.VMEM)
    return pl.pallas_call(
        kernel,
        out_shape=outs,
        in_specs=[smem] * scalars + [vmem] * (len(operands) - scalars),
        out_specs=[vmem] * len(outs),
        scratch_shapes=list(scratch),
        compiler_params=pltpu.CompilerParams(vmem_limit_bytes=48 * 1024 * 1024),
        cost_estimate=pl.CostEstimate(flops=cost[0], bytes_accessed=cost[1], transcendentals=cost[2]),
    )(*operands)


def body(
    coarse, row_map, row_frac, col_map, col_frac, noise_init, noise_churn,
    w_state, w_cond, w_expand, w_project, w_levels, w_final,
):
    lat_index = lax.axis_index("lat")
    lon_index = lax.axis_index("lon")
    place = jnp.stack([lat_index, lon_index]).astype(jnp.int32)
    rings = {}
    for axis in ("lat", "lon"):
        size = lax.axis_size(axis)
        rings[axis] = (
            [((i + 1) % size, i) for i in range(size)],
            [(i, (i + 1) % size) for i in range(size)],
        )

    def swap(axis, to_before, to_after):
        down, up = rings[axis]
        from_before = lax.ppermute(to_after, axis, up)
        from_after = lax.ppermute(to_before, axis, down)
        return from_before, from_after

    def columns(values):
        wide = jnp.concatenate([values[-MARGIN:], values, values[:MARGIN]])
        return lax.dynamic_slice(wide, (lon_index * TILE_COLS,), (PATCH_COLS,)).reshape(1, PATCH_COLS)

    msg = shape((192, 128), BF16)
    to_upper, to_lower, own, own_coarse = call(
        pack_rows_kernel,
        (noise_init, noise_churn, coarse.transpose(2, 1, 0)),
        [msg, msg, shape((2, 192, 128), F32), shape((96, 128), F32)],
        [pltpu.VMEM((2, 192, 128), F32)],
    )
    from_upper, from_lower = swap("lat", to_upper, to_lower)
    wide_msg = shape((288, 128), BF16)
    to_left, to_right, strip, coarse_strip = call(
        pack_cols_kernel,
        (from_upper, from_lower, own, own_coarse),
        [wide_msg, wide_msg, shape((2, ROWS, 128), F32), shape((288, 128), F32)],
    )
    from_left, from_right = swap("lon", to_left, to_right)

    weights = call(
        prepare_kernel,
        (
            w_state.T, w_expand, w_project, w_levels, w_final, jnp.asarray(np.eye(128), BF16),
            jnp.asarray(PICK_IN, BF16), jnp.asarray(PICK_OUT, BF16),
        ),
        [
            shape((48, 256), BF16), shape((256, 256), BF16), shape((256, 256), BF16),
            shape((4, 1152, 128), BF16), shape((48, 256), BF16),
        ],
        [pltpu.VMEM((36, 128), F32)],
        cost=(2 * 36 * 128**3, 4 << 20, 0),
    )
    mean_w = np.zeros((256, 256), np.float32)
    mean_w[:128, :128] = mean_w[128:, 128:] = 4.0 / 128.0
    constants = [jnp.asarray(c, BF16) for c in (PERM, BACK, mean_w, POOL, GROW)]
    field = shape((ROWS, 128), F32)
    cost = (5 * 10**9, 8 << 20, 3 * 10**6)
    den, to_upper, to_lower, state, churn, fields, colmix = call(
        first_kernel,
        (
            place, row_map, row_frac, columns(col_map), columns(col_frac),
            strip, coarse_strip, from_left, from_right, w_cond.T, *weights, *constants,
        ),
        [
            field, msg, msg, field, field,
            shape((18, COARSE_SLOTS, 128), F32), shape((COARSE_SLOTS, 128), BF16),
        ],
        [pltpu.VMEM((18, COARSE_SLOTS, 128), F32)] + CORE_SCRATCH,
        scalars=3,
        cost=cost,
    )
    from_upper, from_lower = swap("lat", to_upper, to_lower)
    total, to_left, to_right = call(
        add_rows_kernel, (place, den, from_upper, from_lower), [field, msg, msg], scalars=1
    )
    from_left, from_right = swap("lon", to_left, to_right)
    short_msg = shape((96, 128), BF16)
    den, to_upper, to_lower, raised = call(
        second_kernel,
        (
            place, row_map, row_frac, total, from_left, from_right, state, churn, fields, colmix,
            *weights, *constants,
        ),
        [field, short_msg, short_msg, field],
        CORE_SCRATCH,
        scalars=3,
        cost=cost,
    )
    from_upper, from_lower = swap("lat", to_upper, to_lower)
    total, to_left, to_right = call(
        add_tile_rows_kernel,
        (place, den, from_upper, from_lower),
        [shape((192, 128), F32), short_msg, short_msg],
        scalars=1,
    )
    from_left, from_right = swap("lon", to_left, to_right)
    (final,) = call(
        finish_kernel,
        (place, total, from_left, from_right, raised),
        [shape((4, TILE_ROWS, TILE_COLS), F32)],
        [pltpu.VMEM((192, 128), F32)],
        scalars=1,
    )
    return final


def solution(mesh):
    sharded = P(None, "lat", "lon")
    return jax.shard_map(
        body,
        mesh=mesh,
        in_specs=(sharded, P(), P(), P(), P(), sharded, sharded) + (P(),) * 6,
        out_specs=sharded,
        check_vma=False,
    )
```

```python
import math

import jax
import jax.numpy as jnp
import numpy as np
from jax import lax
from jax.experimental import pallas as pl
from jax.experimental.pallas import tpu as pltpu
from jax.sharding import PartitionSpec as P

MARGIN = 24
TILE_ROWS, TILE_COLS = 48, 80
PATCH_ROWS, PATCH_COLS = 96, 128
CH = 128
ROWS = 4 * PATCH_ROWS
PAIRS = PATCH_ROWS // 2
FIRST_BATCH, LAST_BATCH = 16, 24
LEVEL1_BATCH, LEVEL2_BATCH = 24, 24
SIDE = 16
COARSE_SLOTS = 48

sigma_data = 0.5
level_first = 4.0
level_second = 1.0
level_raised = 1.5
level_final = 0.25
epsilon = 1e-06

F32 = jnp.float32
BF16 = jnp.bfloat16


def _constants():
    place = np.arange(128)
    column = 8 * (place % 16) + place // 16
    perm = (column[:, None] == np.arange(128)[None, :]).astype(np.float32)
    back = []
    for shift in range(3):
        one = (column[:, None] == (np.arange(128) + shift - 1)[None, :]).astype(np.float32)
        back += [one, one]
    back = np.concatenate(back, 0)
    pick_in = np.zeros((2, 48, 36), np.float32)
    pick_out = np.zeros((2, 48, 36), np.float32)
    for pi in range(2):
        for dc in range(3):
            for pp in range(4):
                for e in range(4):
                    dr = pp - pi
                    if 0 <= dr <= 2:
                        pick_in[pi, dc * 16 + pp * 4 + e, (3 * dr + dc) * 4 + e] = 1.0
                    dr = pi + 2 - pp
                    if 0 <= dr <= 2:
                        pick_out[pi, dc * 16 + pp * 4 + e, (3 * dr + dc) * 4 + e] = 1.0
    pool = np.zeros((9, 6, 8, 12, 16), np.float32)
    for dr in range(3):
        for dc in range(3):
            for r in range(6):
                for c in range(8):
                    rr, cc = r + dr - 1, c + dc - 1
                    if 0 <= rr < 6 and 0 <= cc < 8:
                        pool[3 * dr + dc, r, c, 2 * rr : 2 * rr + 2, 2 * cc : 2 * cc + 2] = 0.25
    pool = pool.reshape(432, 192)
    grow = np.zeros((12, 16, 6, 8), np.float32)
    for r in range(12):
        for c in range(16):
            grow[r, c, r // 2, c // 2] = 1.0
    grow = grow.reshape(192, 48)
    return perm, back, pick_in, pick_out, pool, grow


PERM, BACK, PICK_IN, PICK_OUT, POOL, GROW = _constants()


def dot_nt(a, b):
    return lax.dot_general(a, b, (((1,), (1,)), ((), ())), preferred_element_type=F32)


def dot_nn(a, b):
    return jnp.dot(a, b, preferred_element_type=F32)


def lanes(shape):
    return lax.broadcasted_iota(jnp.int32, shape, 1)


def roll_lanes(value, amount):
    amount = amount % 128
    return value if amount == 0 else pltpu.roll(value, amount, 1)


def prepare_kernel(
    w_state, w_expand, w_project, w_levels, w_final, eye, pick_in, pick_out,
    first_w, expand_w, project_w, level_w, final_w, flat_final,
):
    unit = eye[...]
    for k in range(9):
        flat_final[4 * k : 4 * k + 4, :] = w_final[k].astype(F32)
    final_rows = flat_final[...].astype(BF16)
    state_rows = w_state[...]
    for pi in range(2):
        part = slice(pi * 128, pi * 128 + 128)
        first_w[:, part] = dot_nn(pick_in[pi], state_rows).astype(BF16)
        final_w[:, part] = dot_nn(pick_out[pi], final_rows).astype(BF16)
    zero = jnp.zeros((128, 128), BF16)
    for source, target, factor in ((w_expand, expand_w, 0.5), (w_project, project_w, 1.0)):
        block = (dot_nt(unit, source[...]) * factor).astype(BF16)
        target[0:128, 0:128] = block
        target[128:256, 128:256] = block
        target[0:128, 128:256] = zero
        target[128:256, 0:128] = zero
    for level in range(4):
        for k in range(9):
            level_w[level, k * 128 : k * 128 + 128, :] = dot_nt(unit, w_levels[level, k]).astype(BF16)


def pack_rows_kernel(noise_init, noise_churn, coarse, to_upper, to_lower, own, own_coarse, padded):
    for which, noise in enumerate((noise_init, noise_churn)):
        for e in range(4):
            padded[which, pl.ds(e, TILE_ROWS, stride=4), 0:TILE_COLS] = noise[e]
    own_coarse[...] = jnp.zeros((96, 128), F32)
    for k in range(10):
        own_coarse[pl.ds(k, 6, stride=16), 0:40] = coarse[k].astype(F32)
    lane = lanes((96, 128))
    placed = roll_lanes(own_coarse[...], 80)
    for which in range(2):
        own[which] = padded[which]
        for target, start in ((to_upper, 0), (to_lower, 96)):
            part = padded[which, start : start + 96, :]
            if which == 0:
                part = jnp.where(lane < 80, part, placed)
            target[which * 96 : which * 96 + 96, :] = part.astype(BF16)


def pack_cols_kernel(from_upper, from_lower, own, own_coarse, to_left, to_right, strip, coarse_strip):
    lane = lanes((192, 128))
    for which in range(2):
        rows = slice(which * 96, which * 96 + 96)
        strip[which, 0:96, :] = roll_lanes(from_upper[rows, :].astype(F32), MARGIN)
        strip[which, 96:288, :] = roll_lanes(own[which], MARGIN)
        strip[which, 288:384, :] = roll_lanes(from_lower[rows, :].astype(F32), MARGIN)
    left = right = None
    for group in range(4):
        part = strip[group // 2, (group % 2) * 192 : (group % 2) * 192 + 192, :]
        for_left = roll_lanes(part, 32 * group - 24)
        for_right = roll_lanes(part, 32 * group - 80)
        inside = (lane >= 32 * group) & (lane < 32 * group + 32)
        left = for_left if group == 0 else jnp.where(inside, for_left, left)
        right = for_right if group == 0 else jnp.where(inside, for_right, right)
    to_left[0:192, :] = left.astype(BF16)
    to_right[0:192, :] = right.astype(BF16)
    narrow = lanes((96, 128))
    above = roll_lanes(from_upper[0:96, :].astype(F32), -80)
    middle = own_coarse[...]
    below = roll_lanes(from_lower[0:96, :].astype(F32), -80)
    for index, part in enumerate((above, middle, below)):
        coarse_strip[index * 96 : index * 96 + 96, :] = jnp.where(narrow < 40, part, 0.0)
    packed = jnp.where(narrow < 40, above, jnp.where(narrow < 80, roll_lanes(middle, 40), roll_lanes(below, 80)))
    to_left[192:288, :] = packed.astype(BF16)
    to_right[192:288, :] = packed.astype(BF16)


def pad_store(target, row, pooled, groups):
    rows = pooled.shape[0]
    place = lax.broadcasted_iota(jnp.int32, (SIDE, 128), 0)
    target[pl.ds(row + 1, rows), SIDE : SIDE + groups * SIDE, :] = pooled.reshape(
        rows, groups * SIDE, 128
    ).astype(BF16)
    for r in range(rows):
        before = pltpu.roll(pooled[r, groups - 1], 1, 0)
        after = pltpu.roll(pooled[r, 0], SIDE - 1, 0)
        target[row + 1 + r, 0:SIDE, :] = jnp.where(place == 0, 0.0, before).astype(BF16)
        target[row + 1 + r, SIDE + groups * SIDE : 2 * SIDE + groups * SIDE, :] = jnp.where(
            place == SIDE - 1, 0.0, after
        ).astype(BF16)


def halve(values, rows, groups):
    grouped = values.reshape(rows // 2, 2, groups // 2, 2, SIDE, 128)
    return 0.25 * (
        (grouped[:, 0, :, 0] + grouped[:, 0, :, 1]) + (grouped[:, 1, :, 0] + grouped[:, 1, :, 1])
    )


def norm_silu(values, mean_w):
    squares = dot_nn((values * values).astype(BF16), mean_w)
    half = values * lax.rsqrt(squares + 4.0 * epsilon)
    return half + half * jnp.tanh(half)


def conv_rows(source, weight, row, rows, groups):
    taps = [
        source[pl.ds(row + dr, rows), dc * SIDE : dc * SIDE + groups * SIDE, :].reshape(
            rows * groups * SIDE, 128
        )
        for dr in range(3)
        for dc in range(3)
    ]
    return dot_nn(jnp.concatenate(taps, axis=1), weight)


CORE_SCRATCH = [
    pltpu.VMEM((3, 400, 128), F32),
    pltpu.VMEM((PAIRS, 128, 256), BF16),
    pltpu.VMEM((50, 96, 128), BF16),
    pltpu.VMEM((26, 64, 128), BF16),
    pltpu.VMEM((14, 48, 128), BF16),
    pltpu.VMEM((48, 64, 128), F32),
    pltpu.VMEM((24, 32, 128), F32),
    pltpu.VMEM((3, 392, 128), F32),
    pltpu.VMEM((3, 400, 128), F32),
]


def denoise(
    state, colmix, coarse_fields, lat, row_map, row_frac, weights, constants, scratch, noise_level, out
):
    first_w, expand_w, project_w, level_w, final_w = weights
    perm, back, mean_w, pool, grow = constants
    scaled, hidden, pooled1, pooled2, pooled3, level1, level2, taps_a, taps_b = scratch
    total_sq = noise_level * noise_level + sigma_data * sigma_data

    for shift in range(3):
        scaled[shift, 0:8, :] = jnp.zeros((8, 128), F32)
        scaled[shift, 384:400, :] = jnp.zeros((16, 128), F32)
        taps_a[shift, 384:392, :] = jnp.zeros((8, 128), F32)
        taps_b[shift, 0:8, :] = jnp.zeros((8, 128), F32)
    base = state[...] * (1.0 / math.sqrt(total_sq))
    lane = lanes((ROWS, 128))
    scaled[0, 4 : 4 + ROWS, :] = jnp.where(lane == 0, 0.0, pltpu.roll(base, 1, 1))
    scaled[1, 4 : 4 + ROWS, :] = base
    scaled[2, 4 : 4 + ROWS, :] = jnp.where(lane == 127, 0.0, pltpu.roll(base, 127, 1))
    for buffer, rows in ((pooled1, 50), (pooled2, 26), (pooled3, 14)):
        blank = jnp.zeros(buffer.shape[1:], BF16)
        buffer[0] = blank
        buffer[rows - 1] = blank

    def coarse_row(p):
        y = lat * TILE_ROWS - MARGIN + p
        inside = (y >= 0) & (y < 8 * TILE_ROWS)
        y = jnp.clip(y, 0, 8 * TILE_ROWS - 1)
        at = jnp.clip(row_map[y] - (lat * 6 - 6), 0, 16)
        fraction = row_frac[y]
        near = jnp.where(inside, 1.0 - fraction, 0.0)
        far = jnp.where(inside, fraction, 0.0)
        return near * coarse_fields[at] + far * coarse_fields[at + 1]

    def first(c, carry):
        pre = []
        for k in range(FIRST_BATCH):
            i = FIRST_BATCH * c + k
            row = pl.multiple_of(8 * FIRST_BATCH * c, 8) + 8 * k
            columns = [scaled[shift, pl.ds(row, 16), :].astype(BF16) for shift in range(3)]
            turned = dot_nt(perm[...], jnp.concatenate(columns + [colmix[...]], axis=0)).astype(BF16)
            fields = jnp.concatenate([coarse_row(2 * i), coarse_row(2 * i + 1)], axis=1).astype(BF16)
            pre.append(dot_nn(turned, jnp.concatenate([first_w[...], fields], axis=0)))
        act = norm_silu(jnp.concatenate(pre, axis=0), mean_w[...])
        hidden[pl.ds(FIRST_BATCH * c, FIRST_BATCH)] = act.astype(BF16).reshape(FIRST_BATCH, 128, 256)
        summed = (act[:, 0:128] + act[:, 128:256]).reshape(FIRST_BATCH, 4, 2, SIDE, 128)
        pad_store(pooled1, FIRST_BATCH * c, 0.25 * (summed[:, :, 0] + summed[:, :, 1]), 4)
        return carry

    lax.fori_loop(0, PAIRS // FIRST_BATCH, first, 0)

    mean_one = mean_w[0:128, 0:128]

    def one(c, carry):
        act = norm_silu(conv_rows(pooled1, level_w[0], LEVEL1_BATCH * c, LEVEL1_BATCH, 4), mean_one)
        level1[pl.ds(LEVEL1_BATCH * c, LEVEL1_BATCH)] = act.reshape(LEVEL1_BATCH, 64, 128)
        pad_store(pooled2, LEVEL1_BATCH // 2 * c, halve(act, LEVEL1_BATCH, 4), 2)
        return carry

    lax.fori_loop(0, 48 // LEVEL1_BATCH, one, 0)

    def two(c, carry):
        act = norm_silu(conv_rows(pooled2, level_w[1], LEVEL2_BATCH * c, LEVEL2_BATCH, 2), mean_one)
        level2[pl.ds(LEVEL2_BATCH * c, LEVEL2_BATCH)] = act.reshape(LEVEL2_BATCH, 32, 128)
        pad_store(pooled3, LEVEL2_BATCH // 2 * c, halve(act, LEVEL2_BATCH, 2), 1)
        return carry

    lax.fori_loop(0, 24 // LEVEL2_BATCH, two, 0)

    act3 = norm_silu(conv_rows(pooled3, level_w[2], 0, 12, 1), mean_one)
    shifted = dot_nn(pool[...], act3.astype(BF16)).astype(BF16)
    act4 = norm_silu(
        dot_nn(jnp.concatenate([shifted[48 * k : 48 * k + 48] for k in range(9)], axis=1), level_w[3]),
        mean_one,
    )
    merged3 = act3 + dot_nn(grow[...], act4.astype(BF16))
    merged2 = level2[...].reshape(12, 2, 2, SIDE, 128) + merged3.reshape(12, 1, 1, SIDE, 128)
    level2[...] = merged2.reshape(24, 32, 128)

    def last(c, carry):
        merged = []
        for k in range(LAST_BATCH):
            i = LAST_BATCH * c + k
            coarse2 = level2[i // 2].reshape(2, 1, SIDE, 128)
            merged1 = level1[i].reshape(2, 2, SIDE, 128) + coarse2
            merged1 = merged1.reshape(4, 1, SIDE, 128)
            merged1 = jnp.concatenate([merged1, merged1], axis=1).reshape(128, 128)
            merged.append(jnp.concatenate([merged1, merged1], axis=1))
        merged = jnp.concatenate(merged, axis=0)
        before = hidden[pl.ds(LAST_BATCH * c, LAST_BATCH)].reshape(LAST_BATCH * 128, 256)
        joined = (before.astype(F32) + merged).astype(BF16)
        half = dot_nn(joined, expand_w[...])
        inner = (half + half * jnp.tanh(half)).astype(BF16)
        mixed = (joined.astype(F32) + dot_nn(inner, project_w[...])).astype(BF16)
        for k in range(LAST_BATCH):
            taps = dot_nt(final_w[...], mixed[128 * k : 128 * k + 128])
            row = pl.multiple_of(8 * LAST_BATCH * c, 8) + 8 * k
            for shift in range(3):
                taps_a[shift, pl.ds(row, 8), :] = taps[16 * shift : 16 * shift + 8]
                taps_b[shift, pl.ds(row + 8, 8), :] = taps[16 * shift + 8 : 16 * shift + 16]
        return carry

    lax.fori_loop(0, PAIRS // LAST_BATCH, last, 0)

    parts = []
    for shift in range(3):
        total = taps_a[shift, 4 : 4 + ROWS, :] + taps_b[shift, 4 : 4 + ROWS, :]
        upper = total.astype(BF16)
        parts += [upper, (total - upper.astype(F32)).astype(BF16)]
    refined = dot_nn(jnp.concatenate(parts, axis=1), back[...])
    skip_scale = sigma_data * sigma_data / total_sq
    out_scale = noise_level * sigma_data / math.sqrt(total_sq)
    out[...] = skip_scale * state[...] + out_scale * refined


def inside_rows(lat):
    row = lax.broadcasted_iota(jnp.int32, (ROWS, 128), 0)
    first = jnp.where(lat == 0, 4 * MARGIN, 0)
    last = jnp.where(lat == 7, ROWS - 4 * MARGIN, ROWS)
    return (row >= first) & (row < last)


def send_rows(lat, den, to_upper, to_lower, count):
    above = jnp.where(lat > 0, 0.5, 0.0)
    below = jnp.where(lat < 7, 0.5, 0.0)
    to_upper[...] = (above * den[0:count, :]).astype(BF16)
    to_lower[...] = (below * den[ROWS - count : ROWS, :]).astype(BF16)
    half = ROWS // 2
    den[0:half, :] = (1.0 - above) * den[0:half, :]
    den[half:ROWS, :] = (1.0 - below) * den[half:ROWS, :]


def first_kernel(
    place, row_map, row_frac, col_map, col_frac, strip, coarse_strip, from_left, from_right, w_cond,
    first_w, expand_w, project_w, level_w, final_w, perm, back, mean_w, pool, grow,
    den, to_upper, to_lower, state, churn, fields, colmix,
    window, *scratch,
):
    lat, lon = place[0], place[1]
    lane = lanes((192, 128))
    inside = inside_rows(lat)
    for which, target in enumerate((state, churn)):
        for part in range(2):
            group = 2 * which + part
            rows = slice(part * 192, part * 192 + 192)
            left = roll_lanes(from_left[0:192, :].astype(F32), -32 * group)
            right = roll_lanes(from_right[0:192, :].astype(F32), 104 - 32 * group)
            target[rows, :] = jnp.where(lane < 24, left, jnp.where(lane < 104, strip[which, rows, :], right))
    state[...] = jnp.where(inside, level_first * state[...], 0.0)

    narrow = lanes((96, 128))
    for t, source in enumerate((from_left, None, from_right)):
        for part in range(3):
            if source is None:
                rows = coarse_strip[part * 96 : part * 96 + 96, :]
            else:
                rows = roll_lanes(source[192:288, :].astype(F32), -40 * part)
            for j in range(6):
                window[part * 6 + j, t * 16 : t * 16 + 16, :] = rows[j * 16 : j * 16 + 16]
    stacked = window[...].reshape(18 * COARSE_SLOTS, 128)[:, 0:40].astype(BF16)
    fields[...] = dot_nn(stacked, w_cond[...]).reshape(18, COARSE_SLOTS, 128)

    begin = lon * TILE_COLS - MARGIN
    begin = jnp.where(begin < 0, begin + 32 * TILE_COLS, begin)
    row, skip = begin // 128, begin % 128
    after = jnp.where(row == 19, 0, row + 1)
    turn = jnp.where(skip == 0, 0, 128 - skip)
    front = lanes((1, 128)) < 128 - skip

    def stretch(ref):
        return jnp.where(
            front, pltpu.roll(ref[pl.ds(row, 1), :], turn, 1), pltpu.roll(ref[pl.ds(after, 1), :], turn, 1)
        )

    offset = stretch(col_map) - (10 * lon - 10)
    offset = jnp.where(offset < 0, offset + 320, offset)
    offset = jnp.where(offset >= 320, offset - 320, offset)
    slot = lax.broadcasted_iota(jnp.int32, (COARSE_SLOTS, 128), 0)
    tile = jnp.where(slot >= 32, 2, jnp.where(slot >= 16, 1, 0))
    column = jnp.where(slot - 16 * tile < 10, slot - 6 * tile, -1)
    fraction = stretch(col_frac)
    mix = jnp.where(column == offset, 1.0 - fraction, 0.0) + jnp.where(column == offset + 1, fraction, 0.0)
    colmix[...] = mix.astype(BF16)

    denoise(
        state, colmix, fields, lat, row_map, row_frac,
        (first_w, expand_w, project_w, level_w, final_w), (perm, back, mean_w, pool, grow),
        scratch, level_first, den,
    )
    send_rows(lat, den, to_upper, to_lower, 192)


def add_rows_kernel(den, from_upper, from_lower, total, to_left, to_right):
    top = den[0:192, :] + from_upper[...].astype(F32)
    bottom = den[192:384, :] + from_lower[...].astype(F32)
    total[0:192, :] = top
    total[192:384, :] = bottom
    lane = lanes((192, 128))
    to_left[...] = jnp.where(lane < 64, top, roll_lanes(bottom, 64)).astype(BF16)
    to_right[...] = jnp.where(lane < 64, roll_lanes(top, -80), roll_lanes(bottom, 64 - 80)).astype(BF16)


def second_kernel(
    place, row_map, row_frac, total, from_left, from_right, state, churn, fields, colmix,
    first_w, expand_w, project_w, level_w, final_w, perm, back, mean_w, pool, grow,
    den, to_upper, to_lower, raised,
    *scratch,
):
    lat = place[0]
    lane = lanes((192, 128))
    edge = (lane < 48) | (lane >= 80)
    left = from_left[...].astype(F32)
    right = from_right[...].astype(F32)
    inside = inside_rows(lat)
    for part in range(2):
        rows = slice(part * 192, part * 192 + 192)
        from_l = roll_lanes(left, -64 * part)
        from_r = roll_lanes(right, 80 - 64 * part)
        summed = total[rows, :] + jnp.where(lane < 48, from_l, jnp.where(lane >= 80, from_r, 0.0))
        blended = summed * jnp.where(edge, 0.5, 1.0)
        value = state[rows, :]
        value = value + (level_second - level_first) / level_first * (value - blended)
        value = value + math.sqrt(level_raised * level_raised - level_second * level_second) * churn[rows, :]
        raised[rows, :] = value
    raised[...] = jnp.where(inside, raised[...], 0.0)
    denoise(
        raised, colmix, fields, lat, row_map, row_frac,
        (first_w, expand_w, project_w, level_w, final_w), (perm, back, mean_w, pool, grow),
        scratch, level_raised, den,
    )
    send_rows(lat, den, to_upper, to_lower, 96)


def add_tile_rows_kernel(den, from_upper, from_lower, total, to_left, to_right):
    top = den[96:192, :] + from_upper[...].astype(F32)
    bottom = den[192:288, :] + from_lower[...].astype(F32)
    total[0:96, :] = top
    total[96:192, :] = bottom
    lane = lanes((96, 128))
    to_left[...] = jnp.where(lane < 64, top, roll_lanes(bottom, 64)).astype(BF16)
    to_right[...] = jnp.where(lane < 64, roll_lanes(top, -104), roll_lanes(bottom, 64 - 104)).astype(BF16)


def finish_kernel(total, from_left, from_right, raised, out, rows_ref):
    lane = lanes((96, 128))
    edge = (lane < 48) | (lane >= 80)
    left = from_left[...].astype(F32)
    right = from_right[...].astype(F32)
    for part in range(2):
        rows = slice(part * 96, part * 96 + 96)
        from_l = roll_lanes(left, 24 - 64 * part)
        from_r = roll_lanes(right, 80 - 64 * part)
        use_l = (lane >= 24) & (lane < 48)
        use_r = (lane >= 80) & (lane < 104)
        summed = total[rows, :] + jnp.where(use_l, from_l, jnp.where(use_r, from_r, 0.0))
        blended = summed * jnp.where(edge, 0.5, 1.0)
        value = raised[96 + part * 96 : 192 + part * 96, :]
        value = value + (level_final - level_raised) / level_raised * (value - blended)
        rows_ref[rows, :] = roll_lanes(value, -24)
    for e in range(4):
        out[e] = rows_ref[pl.ds(e, TILE_ROWS, stride=4), 0:TILE_COLS]


def shape(dims, dtype):
    return jax.ShapeDtypeStruct(dims, dtype)


def call(kernel, operands, outs, scratch=(), scalars=0, cost=(0, 0, 0), room=40):
    smem = pl.BlockSpec(memory_space=pltpu.SMEM)
    vmem = pl.BlockSpec(memory_space=pltpu.VMEM)
    return pl.pallas_call(
        kernel,
        out_shape=outs,
        in_specs=[smem] * scalars + [vmem] * (len(operands) - scalars),
        out_specs=[vmem] * len(outs),
        scratch_shapes=list(scratch),
        compiler_params=pltpu.CompilerParams(vmem_limit_bytes=room << 20),
        cost_estimate=pl.CostEstimate(flops=cost[0], bytes_accessed=cost[1], transcendentals=cost[2]),
    )(*operands)


def body(
    coarse, row_map, row_frac, col_map, col_frac, noise_init, noise_churn,
    w_state, w_cond, w_expand, w_project, w_levels, w_final,
):
    lat_index = lax.axis_index("lat")
    lon_index = lax.axis_index("lon")
    place = jnp.stack([lat_index, lon_index]).astype(jnp.int32)
    rings = {}
    for axis in ("lat", "lon"):
        size = lax.axis_size(axis)
        rings[axis] = (
            [((i + 1) % size, i) for i in range(size)],
            [(i, (i + 1) % size) for i in range(size)],
        )

    def swap(axis, to_before, to_after):
        down, up = rings[axis]
        from_before = lax.ppermute(to_after, axis, up)
        from_after = lax.ppermute(to_before, axis, down)
        return from_before, from_after

    msg = shape((192, 128), BF16)
    to_upper, to_lower, own, own_coarse = call(
        pack_rows_kernel,
        (noise_init, noise_churn, coarse.transpose(2, 1, 0)),
        [msg, msg, shape((2, 192, 128), F32), shape((96, 128), F32)],
        [pltpu.VMEM((2, 192, 128), F32)],
        room=60,
    )
    from_upper, from_lower = swap("lat", to_upper, to_lower)
    wide_msg = shape((288, 128), BF16)
    to_left, to_right, strip, coarse_strip = call(
        pack_cols_kernel,
        (from_upper, from_lower, own, own_coarse),
        [wide_msg, wide_msg, shape((2, ROWS, 128), F32), shape((288, 128), F32)],
    )
    from_left, from_right = swap("lon", to_left, to_right)

    weights = call(
        prepare_kernel,
        (
            w_state.T, w_expand, w_project, w_levels, w_final, jnp.asarray(np.eye(128), BF16),
            jnp.asarray(PICK_IN, BF16), jnp.asarray(PICK_OUT, BF16),
        ),
        [
            shape((48, 256), BF16), shape((256, 256), BF16), shape((256, 256), BF16),
            shape((4, 1152, 128), BF16), shape((48, 256), BF16),
        ],
        [pltpu.VMEM((36, 128), F32)],
        cost=(2 * 36 * 128**3, 4 << 20, 0),
        room=60,
    )
    mean_w = np.zeros((256, 256), np.float32)
    mean_w[:128, :128] = mean_w[128:, 128:] = 4.0 / 128.0
    constants = [jnp.asarray(c, BF16) for c in (PERM, BACK, mean_w, POOL, GROW)]
    field = shape((ROWS, 128), F32)
    cost = (5 * 10**9, 8 << 20, 3 * 10**6)
    den, to_upper, to_lower, state, churn, fields, colmix = call(
        first_kernel,
        (
            place, row_map, row_frac, col_map.reshape(20, 128), col_frac.reshape(20, 128),
            strip, coarse_strip, from_left, from_right, w_cond.T, *weights, *constants,
        ),
        [
            field, msg, msg, field, field,
            shape((18, COARSE_SLOTS, 128), F32), shape((COARSE_SLOTS, 128), BF16),
        ],
        [pltpu.VMEM((18, COARSE_SLOTS, 128), F32)] + CORE_SCRATCH,
        scalars=3,
        cost=cost,
    )
    from_upper, from_lower = swap("lat", to_upper, to_lower)
    total, to_left, to_right = call(
        add_rows_kernel, (den, from_upper, from_lower), [field, msg, msg]
    )
    from_left, from_right = swap("lon", to_left, to_right)
    short_msg = shape((96, 128), BF16)
    den, to_upper, to_lower, raised = call(
        second_kernel,
        (
            place, row_map, row_frac, total, from_left, from_right, state, churn, fields, colmix,
            *weights, *constants,
        ),
        [field, short_msg, short_msg, field],
        CORE_SCRATCH,
        scalars=3,
        cost=cost,
    )
    from_upper, from_lower = swap("lat", to_upper, to_lower)
    total, to_left, to_right = call(
        add_tile_rows_kernel,
        (den, from_upper, from_lower),
        [shape((192, 128), F32), short_msg, short_msg],
    )
    from_left, from_right = swap("lon", to_left, to_right)
    (final,) = call(
        finish_kernel,
        (total, from_left, from_right, raised),
        [shape((4, TILE_ROWS, TILE_COLS), F32)],
        [pltpu.VMEM((192, 128), F32)],
    )
    return final


def solution(mesh):
    sharded = P(None, "lat", "lon")
    return jax.shard_map(
        body,
        mesh=mesh,
        in_specs=(sharded, P(), P(), P(), P(), sharded, sharded) + (P(),) * 6,
        out_specs=sharded,
        check_vma=False,
    )
```

```python
import math

import jax
import jax.numpy as jnp
import numpy as np
from jax import lax
from jax.experimental import pallas as pl
from jax.experimental.pallas import tpu as pltpu
from jax.sharding import PartitionSpec as P

MARGIN = 24
TILE_ROWS, TILE_COLS = 48, 80
PATCH_ROWS, PATCH_COLS = 96, 128
CH = 128
ROWS = 4 * PATCH_ROWS
PAIRS = PATCH_ROWS // 2
FIRST_BATCH, LAST_BATCH = 16, 24
LEVEL1_BATCH, COND_BATCH = 12, 8
SIDE = 16
COARSE_SLOTS = 48

sigma_data = 0.5
level_first = 4.0
level_second = 1.0
level_raised = 1.5
level_final = 0.25
epsilon = 1e-06

F32 = jnp.float32
BF16 = jnp.bfloat16


def _constants():
    place = np.arange(128)
    column = 8 * (place % 16) + place // 16
    shifts = [
        (np.arange(128)[:, None] == (column + shift - 1)[None, :]).astype(np.float32) for shift in range(3)
    ]
    shifts = np.concatenate(shifts, 1)
    back = []
    for shift in range(3):
        one = (column[:, None] == (np.arange(128) + shift - 1)[None, :]).astype(np.float32)
        back += [one, one]
    back = np.concatenate(back, 0)
    pick_in = np.zeros((2, 48, 128), np.float32)
    pick_out = np.zeros((2, 48, 128), np.float32)
    pick_cond = np.zeros((2, 80, 128), np.float32)
    for pi in range(2):
        pick_cond[pi, pi * 40 + np.arange(40), np.arange(40)] = 1.0
        for dc in range(3):
            for pp in range(4):
                for e in range(4):
                    dr = pp - pi
                    if 0 <= dr <= 2:
                        pick_in[pi, dc * 16 + pp * 4 + e, (3 * dr + dc) * 4 + e] = 1.0
                    dr = pi + 2 - pp
                    if 0 <= dr <= 2:
                        pick_out[pi, dc * 16 + pp * 4 + e, (3 * dr + dc) * 4 + e] = 1.0
    picks = np.concatenate([v.reshape(-1, 128) for v in (pick_in, pick_cond, pick_out, np.eye(128))], 0)
    pool = np.zeros((9, 6, 8, 12, 16), np.float32)
    for dr in range(3):
        for dc in range(3):
            for r in range(6):
                for c in range(8):
                    rr, cc = r + dr - 1, c + dc - 1
                    if 0 <= rr < 6 and 0 <= cc < 8:
                        pool[3 * dr + dc, r, c, 2 * rr : 2 * rr + 2, 2 * cc : 2 * cc + 2] = 0.25
    pool = pool.reshape(432, 6, 2, 16).transpose(0, 2, 1, 3).reshape(432, 192)
    grow = np.zeros((12, 16, 6, 8), np.float32)
    for r in range(12):
        for c in range(16):
            grow[r, c, r // 2, c // 2] = 1.0
    grow = grow.reshape(6, 2, 16, 48).transpose(1, 0, 2, 3).reshape(192, 48)
    return shifts, back, picks, pool, grow


SHIFTS, BACK, PICKS, POOL, GROW = _constants()


def dot_nt(a, b):
    return lax.dot_general(a, b, (((1,), (1,)), ((), ())), preferred_element_type=F32)


def dot_nn(a, b):
    return jnp.dot(a, b, preferred_element_type=F32)


def lanes(shape):
    return lax.broadcasted_iota(jnp.int32, shape, 1)


def roll_lanes(value, amount):
    amount = amount % 128
    return value if amount == 0 else pltpu.roll(value, amount, 1)


def prepare_kernel(
    w_state, w_cond, w_expand, w_project, w_levels, w_final, picks,
    first_w, expand_w, project_w, level_w, last_level_w, final_w, flat_final,
):
    unit = picks[352:480, :]
    for k in range(9):
        flat_final[4 * k : 4 * k + 4, :] = w_final[k].astype(F32)
    final_rows = flat_final[...].astype(BF16)
    for pi in range(2):
        part = slice(pi * 128, pi * 128 + 128)
        first_w[0:48, part] = dot_nn(picks[pi * 48 : pi * 48 + 48, 0:36], w_state[...]).astype(BF16)
        first_w[48:128, part] = dot_nn(picks[96 + pi * 80 : 176 + pi * 80, 0:40], w_cond[...]).astype(BF16)
        final_w[:, part] = dot_nn(picks[256 + pi * 48 : 304 + pi * 48, 0:36], final_rows).astype(BF16)
    zero = jnp.zeros((128, 128), BF16)
    for source, target, factor in ((w_expand, expand_w, 0.5), (w_project, project_w, 1.0)):
        block = (dot_nt(unit, source[...]) * factor).astype(BF16)
        target[0:128, 0:128] = block
        target[128:256, 128:256] = block
        target[0:128, 128:256] = zero
        target[128:256, 0:128] = zero
    for level in range(3):
        for dc in range(3):
            level_w[level, (9 + dc) * 128 : (10 + dc) * 128, 0:128] = zero
            level_w[level, dc * 128 : dc * 128 + 128, 128:256] = zero
            for dr in range(3):
                block = dot_nt(unit, w_levels[level, 3 * dr + dc]).astype(BF16)
                for pi in range(2):
                    start = (3 * (dr + pi) + dc) * 128
                    level_w[level, start : start + 128, pi * 128 : pi * 128 + 128] = block
    for k in range(9):
        last_level_w[k * 128 : k * 128 + 128, :] = dot_nt(unit, w_levels[3, k]).astype(BF16)


def pack_rows_kernel(noise_init, noise_churn, coarse, to_upper, to_lower, own, own_coarse, padded):
    for which, noise in enumerate((noise_init, noise_churn)):
        for e in range(4):
            padded[which, pl.ds(e, TILE_ROWS, stride=4), 0:TILE_COLS] = noise[e]
    own_coarse[...] = jnp.zeros((96, 128), F32)
    for k in range(10):
        own_coarse[pl.ds(k, 6, stride=16), 0:40] = coarse[k].astype(F32)
    lane = lanes((96, 128))
    placed = roll_lanes(own_coarse[...], 80)
    for which in range(2):
        own[which] = padded[which]
        for target, start in ((to_upper, 0), (to_lower, 96)):
            part = padded[which, start : start + 96, :]
            if which == 0:
                part = jnp.where(lane < 80, part, placed)
            target[which * 96 : which * 96 + 96, :] = part.astype(BF16)


def pack_cols_kernel(from_upper, from_lower, own, own_coarse, to_left, to_right, strip, coarse_strip):
    lane = lanes((192, 128))
    for which in range(2):
        rows = slice(which * 96, which * 96 + 96)
        strip[which, 0:96, :] = roll_lanes(from_upper[rows, :].astype(F32), MARGIN)
        strip[which, 96:288, :] = roll_lanes(own[which], MARGIN)
        strip[which, 288:384, :] = roll_lanes(from_lower[rows, :].astype(F32), MARGIN)
    left = right = None
    for group in range(4):
        part = strip[group // 2, (group % 2) * 192 : (group % 2) * 192 + 192, :]
        for_left = roll_lanes(part, 32 * group - 24)
        for_right = roll_lanes(part, 32 * group - 80)
        inside = (lane >= 32 * group) & (lane < 32 * group + 32)
        left = for_left if group == 0 else jnp.where(inside, for_left, left)
        right = for_right if group == 0 else jnp.where(inside, for_right, right)
    to_left[0:192, :] = left.astype(BF16)
    to_right[0:192, :] = right.astype(BF16)
    narrow = lanes((96, 128))
    above = roll_lanes(from_upper[0:96, :].astype(F32), -80)
    middle = own_coarse[...]
    below = roll_lanes(from_lower[0:96, :].astype(F32), -80)
    for index, part in enumerate((above, middle, below)):
        coarse_strip[index * 96 : index * 96 + 96, :] = jnp.where(narrow < 40, part, 0.0)
    packed = jnp.where(narrow < 40, above, jnp.where(narrow < 80, roll_lanes(middle, 40), roll_lanes(below, 80)))
    to_left[192:288, :] = packed.astype(BF16)
    to_right[192:288, :] = packed.astype(BF16)


def pad_store(target, row, pooled, groups):
    rows = pooled.shape[0]
    place = lax.broadcasted_iota(jnp.int32, (SIDE, 128), 0)
    target[pl.ds(row + 1, rows), SIDE : SIDE + groups * SIDE, :] = pooled.reshape(
        rows, groups * SIDE, 128
    ).astype(BF16)
    for r in range(rows):
        before = pltpu.roll(pooled[r, groups - 1], 1, 0)
        after = pltpu.roll(pooled[r, 0], SIDE - 1, 0)
        target[row + 1 + r, 0:SIDE, :] = jnp.where(place == 0, 0.0, before).astype(BF16)
        target[row + 1 + r, SIDE + groups * SIDE : 2 * SIDE + groups * SIDE, :] = jnp.where(
            place == SIDE - 1, 0.0, after
        ).astype(BF16)


def halve(values, pairs, groups):
    summed = (values[:, 0:128] + values[:, 128:256]).reshape(pairs, groups // 2, 2, SIDE, 128)
    return 0.25 * (summed[:, :, 0] + summed[:, :, 1])


def norm_silu(values, mean_w):
    squares = dot_nn((values * values).astype(BF16), mean_w)
    half = values * lax.rsqrt(squares + 4.0 * epsilon)
    return half + half * jnp.tanh(half)


def conv_rows(source, weight, pair, pairs, groups):
    taps = [
        jnp.concatenate(
            [
                source[2 * (pair + m) + rr, dc * SIDE : dc * SIDE + groups * SIDE, :]
                for m in range(pairs)
            ],
            axis=0,
        )
        for rr in range(4)
        for dc in range(3)
    ]
    return dot_nn(jnp.concatenate(taps, axis=1), weight)


CORE_SCRATCH = [
    pltpu.VMEM((3, 400, 128), F32),
    pltpu.VMEM((PAIRS, 128, 256), BF16),
    pltpu.VMEM((50, 96, 128), BF16),
    pltpu.VMEM((26, 64, 128), BF16),
    pltpu.VMEM((14, 48, 128), BF16),
    pltpu.VMEM((24, 64, 256), F32),
    pltpu.VMEM((12, 32, 256), F32),
    pltpu.VMEM((3, 392, 128), F32),
    pltpu.VMEM((3, 400, 128), F32),
]


def denoise(state, cond_rows, weights, constants, scratch, noise_level, out):
    first_w, expand_w, project_w, level_w, last_level_w, final_w = weights
    shifts, back, mean_w, pool, grow = constants
    scaled, hidden, pooled1, pooled2, pooled3, level1, level2, taps_a, taps_b = scratch
    total_sq = noise_level * noise_level + sigma_data * sigma_data

    for shift in range(3):
        scaled[shift, 0:8, :] = jnp.zeros((8, 128), F32)
        scaled[shift, 384:400, :] = jnp.zeros((16, 128), F32)
        taps_a[shift, 384:392, :] = jnp.zeros((8, 128), F32)
        taps_b[shift, 0:8, :] = jnp.zeros((8, 128), F32)
    base = (state[...] * (1.0 / math.sqrt(total_sq))).astype(BF16)
    for shift in range(3):
        scaled[shift, 4 : 4 + ROWS, :] = dot_nn(base, shifts[:, shift * 128 : shift * 128 + 128])
    for buffer, rows in ((pooled1, 50), (pooled2, 26), (pooled3, 14)):
        blank = jnp.zeros(buffer.shape[1:], BF16)
        buffer[0] = blank
        buffer[rows - 1] = blank

    def first(c, carry):
        turned = []
        for k in range(FIRST_BATCH):
            row = pl.multiple_of(8 * FIRST_BATCH * c, 8) + 8 * k
            columns = [scaled[shift, pl.ds(row, 16), :].astype(BF16) for shift in range(3)]
            turned.append(jnp.concatenate(columns + [cond_rows[FIRST_BATCH * c + k]], axis=0).T)
        pre = dot_nn(jnp.concatenate(turned, axis=0), first_w[...])
        act = norm_silu(pre, mean_w[...])
        hidden[pl.ds(FIRST_BATCH * c, FIRST_BATCH)] = act.astype(BF16).reshape(FIRST_BATCH, 128, 256)
        summed = (act[:, 0:128] + act[:, 128:256]).reshape(FIRST_BATCH, 4, 2, SIDE, 128)
        pad_store(pooled1, FIRST_BATCH * c, 0.25 * (summed[:, :, 0] + summed[:, :, 1]), 4)
        return carry

    lax.fori_loop(0, PAIRS // FIRST_BATCH, first, 0)

    def one(c, carry):
        act = norm_silu(conv_rows(pooled1, level_w[0], LEVEL1_BATCH * c, LEVEL1_BATCH, 4), mean_w[...])
        level1[pl.ds(LEVEL1_BATCH * c, LEVEL1_BATCH)] = act.reshape(LEVEL1_BATCH, 64, 256)
        pad_store(pooled2, LEVEL1_BATCH * c, halve(act, LEVEL1_BATCH, 4), 2)
        return carry

    lax.fori_loop(0, 24 // LEVEL1_BATCH, one, 0)

    act = norm_silu(conv_rows(pooled2, level_w[1], 0, 12, 2), mean_w[...])
    level2[...] = act.reshape(12, 32, 256)
    pad_store(pooled3, 0, halve(act, 12, 2), 1)

    act3 = norm_silu(conv_rows(pooled3, level_w[2], 0, 6, 1), mean_w[...])
    act3 = jnp.concatenate([act3[:, 0:128], act3[:, 128:256]], axis=0)
    shifted = dot_nn(pool[...], act3.astype(BF16)).astype(BF16)
    act4 = norm_silu(
        dot_nn(jnp.concatenate([shifted[48 * k : 48 * k + 48] for k in range(9)], axis=1), last_level_w[...]),
        mean_w[0:128, 0:128],
    )
    merged3 = act3 + dot_nn(grow[...], act4.astype(BF16))
    for a in range(12):
        start = a % 2 * 96 + a // 2 * SIDE
        above = merged3[start : start + SIDE]
        above = jnp.concatenate([above, above], axis=0)
        level2[a] = level2[a] + jnp.concatenate([above, above], axis=1)

    def last(c, carry):
        merged = []
        for k in range(LAST_BATCH):
            half_of = slice(k % 2 * 128, k % 2 * 128 + 128)
            quarter_of = slice(k // 2 % 2 * 128, k // 2 % 2 * 128 + 128)
            coarse2 = level2[LAST_BATCH // 4 * c + k // 4, :, quarter_of].reshape(2, 1, SIDE, 128)
            merged1 = level1[LAST_BATCH // 2 * c + k // 2, :, half_of].reshape(2, 2, SIDE, 128) + coarse2
            merged1 = merged1.reshape(4, 1, SIDE, 128)
            merged1 = jnp.concatenate([merged1, merged1], axis=1).reshape(128, 128)
            merged.append(jnp.concatenate([merged1, merged1], axis=1))
        merged = jnp.concatenate(merged, axis=0)
        before = hidden[pl.ds(LAST_BATCH * c, LAST_BATCH)].reshape(LAST_BATCH * 128, 256)
        joined = (before.astype(F32) + merged).astype(BF16)
        half = dot_nn(joined, expand_w[...])
        inner = (half + half * jnp.tanh(half)).astype(BF16)
        mixed = (joined.astype(F32) + dot_nn(inner, project_w[...])).astype(BF16)
        for k in range(LAST_BATCH):
            taps = dot_nt(final_w[...], mixed[128 * k : 128 * k + 128])
            row = pl.multiple_of(8 * LAST_BATCH * c, 8) + 8 * k
            for shift in range(3):
                taps_a[shift, pl.ds(row, 8), :] = taps[16 * shift : 16 * shift + 8]
                taps_b[shift, pl.ds(row + 8, 8), :] = taps[16 * shift + 8 : 16 * shift + 16]
        return carry

    lax.fori_loop(0, PAIRS // LAST_BATCH, last, 0)

    parts = []
    for shift in range(3):
        total = taps_a[shift, 4 : 4 + ROWS, :] + taps_b[shift, 4 : 4 + ROWS, :]
        upper = total.astype(BF16)
        parts += [upper, (total - upper.astype(F32)).astype(BF16)]
    refined = dot_nn(jnp.concatenate(parts, axis=1), back[...])
    skip_scale = sigma_data * sigma_data / total_sq
    out_scale = noise_level * sigma_data / math.sqrt(total_sq)
    out[...] = skip_scale * state[...] + out_scale * refined


def inside_rows(lat):
    row = lax.broadcasted_iota(jnp.int32, (ROWS, 128), 0)
    first = jnp.where(lat == 0, 4 * MARGIN, 0)
    last = jnp.where(lat == 7, ROWS - 4 * MARGIN, ROWS)
    return (row >= first) & (row < last)


def send_rows(lat, den, to_upper, to_lower, count):
    above = jnp.where(lat > 0, 0.5, 0.0)
    below = jnp.where(lat < 7, 0.5, 0.0)
    to_upper[...] = (above * den[0:count, :]).astype(BF16)
    to_lower[...] = (below * den[ROWS - count : ROWS, :]).astype(BF16)
    half = ROWS // 2
    den[0:half, :] = (1.0 - above) * den[0:half, :]
    den[half:ROWS, :] = (1.0 - below) * den[half:ROWS, :]


def first_kernel(
    place, row_map, row_frac, col_map, col_frac, strip, coarse_strip, from_left, from_right,
    first_w, expand_w, project_w, level_w, last_level_w, final_w, shifts, back, mean_w, pool, grow,
    den, to_upper, to_lower, state, churn, cond_rows,
    window, coarse_t, *scratch,
):
    lat, lon = place[0], place[1]
    lane = lanes((192, 128))
    inside = inside_rows(lat)
    for which, target in enumerate((state, churn)):
        for part in range(2):
            group = 2 * which + part
            rows = slice(part * 192, part * 192 + 192)
            left = roll_lanes(from_left[0:192, :].astype(F32), -32 * group)
            right = roll_lanes(from_right[0:192, :].astype(F32), 104 - 32 * group)
            target[rows, :] = jnp.where(lane < 24, left, jnp.where(lane < 104, strip[which, rows, :], right))
    state[...] = jnp.where(inside, level_first * state[...], 0.0)

    narrow = lanes((96, 128))
    for t, source in enumerate((from_left, None, from_right)):
        for part in range(3):
            if source is None:
                rows = coarse_strip[part * 96 : part * 96 + 96, :]
            else:
                rows = roll_lanes(source[192:288, :].astype(F32), -40 * part)
            for j in range(6):
                window[part * 6 + j, t * 16 : t * 16 + 16, :] = rows[j * 16 : j * 16 + 16]
    unit = jnp.where(
        lanes((40, 128)) == lax.broadcasted_iota(jnp.int32, (40, 128), 0), 1.0, 0.0
    ).astype(BF16)
    for j in range(18):
        coarse_t[j] = dot_nt(unit, window[j].astype(BF16))

    begin = lon * TILE_COLS - MARGIN
    begin = jnp.where(begin < 0, begin + 32 * TILE_COLS, begin)
    row, skip = begin // 128, begin % 128
    after = jnp.where(row == 19, 0, row + 1)
    turn = jnp.where(skip == 0, 0, 128 - skip)
    front = lanes((1, 128)) < 128 - skip

    def stretch(ref):
        return jnp.where(
            front, pltpu.roll(ref[pl.ds(row, 1), :], turn, 1), pltpu.roll(ref[pl.ds(after, 1), :], turn, 1)
        )

    offset = stretch(col_map) - (10 * lon - 10)
    offset = jnp.where(offset < 0, offset + 320, offset)
    offset = jnp.where(offset >= 320, offset - 320, offset)
    slot = lax.broadcasted_iota(jnp.int32, (COARSE_SLOTS, 128), 0)
    tile = jnp.where(slot >= 32, 2, jnp.where(slot >= 16, 1, 0))
    column = jnp.where(slot - 16 * tile < 10, slot - 6 * tile, -1)
    fraction = stretch(col_frac)
    mix = jnp.where(column == offset, 1.0 - fraction, 0.0) + jnp.where(column == offset + 1, fraction, 0.0)
    mix = dot_nn(mix.astype(BF16), shifts[:, 128:256]).astype(BF16)

    def coarse_row(p):
        y = lat * TILE_ROWS - MARGIN + p
        within = (y >= 0) & (y < 8 * TILE_ROWS)
        y = jnp.clip(y, 0, 8 * TILE_ROWS - 1)
        at = jnp.clip(row_map[y] - (lat * 6 - 6), 0, 16)
        weight = row_frac[y]
        near = jnp.where(within, 1.0 - weight, 0.0)
        far = jnp.where(within, weight, 0.0)
        return near * coarse_t[at] + far * coarse_t[at + 1]

    def interpolate(c, carry):
        rows = [coarse_row(2 * COND_BATCH * c + k) for k in range(2 * COND_BATCH)]
        fine = dot_nn(jnp.concatenate(rows, axis=0).astype(BF16), mix)
        cond_rows[pl.ds(COND_BATCH * c, COND_BATCH)] = fine.astype(BF16).reshape(COND_BATCH, 80, 128)
        return carry

    lax.fori_loop(0, PAIRS // COND_BATCH, interpolate, 0)

    denoise(
        state, cond_rows, (first_w, expand_w, project_w, level_w, last_level_w, final_w),
        (shifts, back, mean_w, pool, grow), scratch, level_first, den,
    )
    send_rows(lat, den, to_upper, to_lower, 192)


def add_rows_kernel(den, from_upper, from_lower, total, to_left, to_right):
    top = den[0:192, :] + from_upper[...].astype(F32)
    bottom = den[192:384, :] + from_lower[...].astype(F32)
    total[0:192, :] = top
    total[192:384, :] = bottom
    lane = lanes((192, 128))
    to_left[...] = jnp.where(lane < 64, top, roll_lanes(bottom, 64)).astype(BF16)
    to_right[...] = jnp.where(lane < 64, roll_lanes(top, -80), roll_lanes(bottom, 64 - 80)).astype(BF16)


def second_kernel(
    place, total, from_left, from_right, state, churn, cond_rows,
    first_w, expand_w, project_w, level_w, last_level_w, final_w, shifts, back, mean_w, pool, grow,
    den, to_upper, to_lower, raised,
    *scratch,
):
    lat = place[0]
    lane = lanes((192, 128))
    edge = (lane < 48) | (lane >= 80)
    left = from_left[...].astype(F32)
    right = from_right[...].astype(F32)
    inside = inside_rows(lat)
    for part in range(2):
        rows = slice(part * 192, part * 192 + 192)
        from_l = roll_lanes(left, -64 * part)
        from_r = roll_lanes(right, 80 - 64 * part)
        summed = total[rows, :] + jnp.where(lane < 48, from_l, jnp.where(lane >= 80, from_r, 0.0))
        blended = summed * jnp.where(edge, 0.5, 1.0)
        value = state[rows, :]
        value = value + (level_second - level_first) / level_first * (value - blended)
        value = value + math.sqrt(level_raised * level_raised - level_second * level_second) * churn[rows, :]
        raised[rows, :] = value
    raised[...] = jnp.where(inside, raised[...], 0.0)
    denoise(
        raised, cond_rows, (first_w, expand_w, project_w, level_w, last_level_w, final_w),
        (shifts, back, mean_w, pool, grow), scratch, level_raised, den,
    )
    send_rows(lat, den, to_upper, to_lower, 96)


def add_tile_rows_kernel(den, from_upper, from_lower, total, to_left, to_right):
    top = den[96:192, :] + from_upper[...].astype(F32)
    bottom = den[192:288, :] + from_lower[...].astype(F32)
    total[0:96, :] = top
    total[96:192, :] = bottom
    lane = lanes((96, 128))
    to_left[...] = jnp.where(lane < 64, top, roll_lanes(bottom, 64)).astype(BF16)
    to_right[...] = jnp.where(lane < 64, roll_lanes(top, -104), roll_lanes(bottom, 64 - 104)).astype(BF16)


def finish_kernel(total, from_left, from_right, raised, out, rows_ref):
    lane = lanes((96, 128))
    edge = (lane < 48) | (lane >= 80)
    left = from_left[...].astype(F32)
    right = from_right[...].astype(F32)
    for part in range(2):
        rows = slice(part * 96, part * 96 + 96)
        from_l = roll_lanes(left, 24 - 64 * part)
        from_r = roll_lanes(right, 80 - 64 * part)
        use_l = (lane >= 24) & (lane < 48)
        use_r = (lane >= 80) & (lane < 104)
        summed = total[rows, :] + jnp.where(use_l, from_l, jnp.where(use_r, from_r, 0.0))
        blended = summed * jnp.where(edge, 0.5, 1.0)
        value = raised[96 + part * 96 : 192 + part * 96, :]
        value = value + (level_final - level_raised) / level_raised * (value - blended)
        rows_ref[rows, :] = roll_lanes(value, -24)
    for e in range(4):
        out[e] = rows_ref[pl.ds(e, TILE_ROWS, stride=4), 0:TILE_COLS]


def shape(dims, dtype):
    return jax.ShapeDtypeStruct(dims, dtype)


def call(kernel, operands, outs, scratch=(), scalars=0, cost=(0, 0, 0), far=()):
    operands = [
        pltpu.with_memory_space_constraint(a, pltpu.HBM) if n in far else a for n, a in enumerate(operands)
    ]
    return pl.pallas_call(
        kernel,
        out_shape=outs,
        in_specs=[pl.BlockSpec(memory_space=pltpu.SMEM)] * scalars
        + [pl.BlockSpec(memory_space=pltpu.VMEM)] * (len(operands) - scalars),
        out_specs=[pl.BlockSpec(memory_space=pltpu.VMEM)] * len(outs),
        scratch_shapes=list(scratch),
        compiler_params=pltpu.CompilerParams(vmem_limit_bytes=40 << 20),
        cost_estimate=pl.CostEstimate(flops=cost[0], bytes_accessed=cost[1], transcendentals=cost[2]),
    )(*operands)


def body(
    coarse, row_map, row_frac, col_map, col_frac, noise_init, noise_churn,
    w_state, w_cond, w_expand, w_project, w_levels, w_final,
):
    lat_index = lax.axis_index("lat")
    lon_index = lax.axis_index("lon")
    place = jnp.stack([lat_index, lon_index]).astype(jnp.int32)
    rings = {}
    for axis in ("lat", "lon"):
        size = lax.axis_size(axis)
        rings[axis] = (
            [((i + 1) % size, i) for i in range(size)],
            [(i, (i + 1) % size) for i in range(size)],
        )

    def swap(axis, to_before, to_after):
        down, up = rings[axis]
        from_before = lax.ppermute(to_after, axis, up)
        from_after = lax.ppermute(to_before, axis, down)
        return from_before, from_after

    msg = shape((192, 128), BF16)
    to_upper, to_lower, own, own_coarse = call(
        pack_rows_kernel,
        (noise_init, noise_churn, coarse.transpose(2, 1, 0)),
        [msg, msg, shape((2, 192, 128), F32), shape((96, 128), F32)],
        [pltpu.VMEM((2, 192, 128), F32)],
        far=(0, 1, 2),
    )
    from_upper, from_lower = swap("lat", to_upper, to_lower)
    wide_msg = shape((288, 128), BF16)
    to_left, to_right, strip, coarse_strip = call(
        pack_cols_kernel,
        (from_upper, from_lower, own, own_coarse),
        [wide_msg, wide_msg, shape((2, ROWS, 128), F32), shape((288, 128), F32)],
    )
    from_left, from_right = swap("lon", to_left, to_right)

    weights = call(
        prepare_kernel,
        (
            w_state.T, w_cond.T, w_expand, w_project, w_levels, w_final, jnp.asarray(PICKS, BF16),
        ),
        [
            shape((128, 256), BF16), shape((256, 256), BF16), shape((256, 256), BF16),
            shape((3, 1536, 256), BF16), shape((1152, 128), BF16), shape((48, 256), BF16),
        ],
        [pltpu.VMEM((36, 128), F32)],
        cost=(2 * 36 * 128**3, 4 << 20, 0),
        far=range(7),
    )
    mean_w = np.zeros((256, 256), np.float32)
    mean_w[:128, :128] = mean_w[128:, 128:] = 4.0 / 128.0
    constants = [jnp.asarray(c, BF16) for c in (SHIFTS, BACK, mean_w, POOL, GROW)]
    field = shape((ROWS, 128), F32)
    cost = (5 * 10**9, 8 << 20, 3 * 10**6)
    den, to_upper, to_lower, state, churn, cond_rows = call(
        first_kernel,
        (
            place, row_map, row_frac, col_map.reshape(20, 128), col_frac.reshape(20, 128),
            strip, coarse_strip, from_left, from_right, *weights, *constants,
        ),
        [
            field, msg, msg, field, field,
            shape((PAIRS, 80, 128), BF16),
        ],
        [pltpu.VMEM((18, COARSE_SLOTS, 128), F32), pltpu.VMEM((18, 40, COARSE_SLOTS), F32)] + CORE_SCRATCH,
        scalars=3,
        cost=cost,
        far=(1, 2, 3, 4, 15, 16, 17, 18, 19),
    )
    from_upper, from_lower = swap("lat", to_upper, to_lower)
    total, to_left, to_right = call(
        add_rows_kernel, (den, from_upper, from_lower), [field, msg, msg]
    )
    from_left, from_right = swap("lon", to_left, to_right)
    short_msg = shape((96, 128), BF16)
    den, to_upper, to_lower, raised = call(
        second_kernel,
        (
            place, total, from_left, from_right, state, churn, cond_rows,
            *weights, *constants,
        ),
        [field, short_msg, short_msg, field],
        CORE_SCRATCH,
        scalars=1,
        cost=cost,
        far=(13, 14, 15, 16, 17),
    )
    from_upper, from_lower = swap("lat", to_upper, to_lower)
    total, to_left, to_right = call(
        add_tile_rows_kernel,
        (den, from_upper, from_lower),
        [shape((192, 128), F32), short_msg, short_msg],
    )
    from_left, from_right = swap("lon", to_left, to_right)
    (final,) = call(
        finish_kernel,
        (total, from_left, from_right, raised),
        [shape((4, TILE_ROWS, TILE_COLS), F32)],
        [pltpu.VMEM((192, 128), F32)],
    )
    return final


def solution(mesh):
    sharded = P(None, "lat", "lon")
    return jax.shard_map(
        body,
        mesh=mesh,
        in_specs=(sharded, P(), P(), P(), P(), sharded, sharded) + (P(),) * 6,
        out_specs=sharded,
        check_vma=False,
    )
```

```python
import math

import jax
import jax.numpy as jnp
import numpy as np
from jax import lax
from jax.experimental import pallas as pl
from jax.experimental.pallas import tpu as pltpu
from jax.sharding import PartitionSpec as P

MARGIN = 24
TILE_ROWS, TILE_COLS = 48, 80
PATCH_ROWS, PATCH_COLS = 96, 128
CH = 128
ROWS = 4 * PATCH_ROWS
PAIRS = PATCH_ROWS // 2
FIRST_BATCH, LAST_BATCH = 48, 48
LEVEL1_BATCH, COND_BATCH = 12, 8
SIDE = 16
COARSE_SLOTS = 48

sigma_data = 0.5
level_first = 4.0
level_second = 1.0
level_raised = 1.5
level_final = 0.25
epsilon = 1e-06

F32 = jnp.float32
BF16 = jnp.bfloat16


def _constants():
    place = np.arange(128)
    column = 8 * (place % 16) + place // 16
    shifts = [
        (np.arange(128)[:, None] == (column + shift - 1)[None, :]).astype(np.float32) for shift in range(3)
    ]
    shifts = np.concatenate(shifts, 1)
    back = []
    for shift in range(3):
        one = (column[:, None] == (np.arange(128) + shift - 1)[None, :]).astype(np.float32)
        back += [one, one]
    back = np.concatenate(back, 0)
    pick_in = np.zeros((2, 48, 128), np.float32)
    pick_out = np.zeros((2, 48, 128), np.float32)
    pick_cond = np.zeros((2, 80, 128), np.float32)
    for pi in range(2):
        pick_cond[pi, pi * 40 + np.arange(40), np.arange(40)] = 1.0
        for dc in range(3):
            for pp in range(4):
                for e in range(4):
                    dr = pp - pi
                    if 0 <= dr <= 2:
                        pick_in[pi, dc * 16 + pp * 4 + e, (3 * dr + dc) * 4 + e] = 1.0
                    dr = pi + 2 - pp
                    if 0 <= dr <= 2:
                        pick_out[pi, dc * 16 + pp * 4 + e, (3 * dr + dc) * 4 + e] = 1.0
    picks = np.concatenate([v.reshape(-1, 128) for v in (pick_in, pick_cond, pick_out, np.eye(128))], 0)
    pool = np.zeros((9, 6, 8, 12, 16), np.float32)
    for dr in range(3):
        for dc in range(3):
            for r in range(6):
                for c in range(8):
                    rr, cc = r + dr - 1, c + dc - 1
                    if 0 <= rr < 6 and 0 <= cc < 8:
                        pool[3 * dr + dc, r, c, 2 * rr : 2 * rr + 2, 2 * cc : 2 * cc + 2] = 0.25
    pool = pool.reshape(432, 6, 2, 16).transpose(0, 2, 1, 3).reshape(432, 192)
    grow = np.zeros((12, 16, 6, 8), np.float32)
    for r in range(12):
        for c in range(16):
            grow[r, c, r // 2, c // 2] = 1.0
    grow = grow.reshape(6, 2, 16, 48).transpose(1, 0, 2, 3).reshape(192, 48)
    return shifts, back, picks, pool, grow


SHIFTS, BACK, PICKS, POOL, GROW = _constants()


def dot_nt(a, b):
    return lax.dot_general(a, b, (((1,), (1,)), ((), ())), preferred_element_type=F32)


def dot_nn(a, b):
    return jnp.dot(a, b, preferred_element_type=F32)


def lanes(shape):
    return lax.broadcasted_iota(jnp.int32, shape, 1)


def choose(flags, first, second):
    return jnp.where(flags[2:3, :] > 0.5, first, second)


def roll_lanes(value, amount):
    amount = amount % 128
    return value if amount == 0 else pltpu.roll(value, amount, 1)


def prepare_kernel(
    w_state, w_cond, w_expand, w_project, w_levels, w_final, picks, shifts, back, mean_w, pool, grow, col_map, col_frac,
    first_w, expand_w, project_w, level_w, last_level_w, final_w,
    own_shifts, own_back, own_mean_w, own_pool, own_grow, own_col_map, own_col_frac, flags, flat_final,
):
    for source, target in (
        (shifts, own_shifts), (back, own_back), (mean_w, own_mean_w), (pool, own_pool), (grow, own_grow),
        (col_map, own_col_map), (col_frac, own_col_frac),
    ):
        target[...] = source[...]
    lat, lon = lax.axis_index("lat"), lax.axis_index("lon")
    row = lax.broadcasted_iota(jnp.int32, (8, 128), 0)
    above = jnp.where(lat > 0, 0.5, 0.0)
    below = jnp.where(lat < 7, 0.5, 0.0)
    odd = jnp.where(lon % 2 == 1, 1.0, 0.0)
    flags[...] = jnp.where(row == 0, above, jnp.where(row == 1, below, odd))
    unit = picks[352:480, :]
    for k in range(9):
        flat_final[4 * k : 4 * k + 4, :] = w_final[k].astype(F32)
    final_rows = flat_final[...].astype(BF16)
    for pi in range(2):
        part = slice(pi * 128, pi * 128 + 128)
        first_w[0:48, part] = dot_nn(picks[pi * 48 : pi * 48 + 48, 0:36], w_state[...]).astype(BF16)
        first_w[48:128, part] = dot_nn(picks[96 + pi * 80 : 176 + pi * 80, 0:40], w_cond[...]).astype(BF16)
        final_w[:, part] = dot_nn(picks[256 + pi * 48 : 304 + pi * 48, 0:36], final_rows).astype(BF16)
    zero = jnp.zeros((128, 128), BF16)
    for source, target, factor in ((w_expand, expand_w, 0.5), (w_project, project_w, 1.0)):
        block = (dot_nt(unit, source[...]) * factor).astype(BF16)
        target[0:128, 0:128] = block
        target[128:256, 128:256] = block
        target[0:128, 128:256] = zero
        target[128:256, 0:128] = zero
    for level in range(3):
        for dc in range(3):
            level_w[level, (9 + dc) * 128 : (10 + dc) * 128, 0:128] = zero
            level_w[level, dc * 128 : dc * 128 + 128, 128:256] = zero
            for dr in range(3):
                block = dot_nt(unit, w_levels[level, 3 * dr + dc]).astype(BF16)
                for pi in range(2):
                    start = (3 * (dr + pi) + dc) * 128
                    level_w[level, start : start + 128, pi * 128 : pi * 128 + 128] = block
    for k in range(9):
        last_level_w[k * 128 : k * 128 + 128, :] = dot_nt(unit, w_levels[3, k]).astype(BF16)


def pack_rows_kernel(noise_init, noise_churn, coarse, to_upper, to_lower, own, own_coarse, padded):
    for which, noise in enumerate((noise_init, noise_churn)):
        for e in range(4):
            padded[which, pl.ds(e, TILE_ROWS, stride=4), 0:TILE_COLS] = noise[e]
    own_coarse[...] = jnp.zeros((96, 128), F32)
    for k in range(10):
        own_coarse[pl.ds(k, 6, stride=16), 0:40] = coarse[k].astype(F32)
    lane = lanes((96, 128))
    placed = roll_lanes(own_coarse[...], 80)
    for which in range(2):
        own[which] = padded[which]
        for target, start in ((to_upper, 0), (to_lower, 96)):
            part = padded[which, start : start + 96, :]
            if which == 0:
                part = jnp.where(lane < 80, part, placed)
            target[which * 96 : which * 96 + 96, :] = part.astype(BF16)


def pack_cols_kernel(flags, from_upper, from_lower, own, own_coarse, to_far, to_near, strip, coarse_strip):
    lane = lanes((192, 128))
    for which in range(2):
        rows = slice(which * 96, which * 96 + 96)
        strip[which, 0:96, :] = roll_lanes(from_upper[rows, :].astype(F32), MARGIN)
        strip[which, 96:288, :] = roll_lanes(own[which], MARGIN)
        strip[which, 288:384, :] = roll_lanes(from_lower[rows, :].astype(F32), MARGIN)
    left = right = None
    for group in range(4):
        part = strip[group // 2, (group % 2) * 192 : (group % 2) * 192 + 192, :]
        for_left = roll_lanes(part, 32 * group - 24)
        for_right = roll_lanes(part, 32 * group - 80)
        inside = (lane >= 32 * group) & (lane < 32 * group + 32)
        left = for_left if group == 0 else jnp.where(inside, for_left, left)
        right = for_right if group == 0 else jnp.where(inside, for_right, right)
    to_near[0:192, :] = choose(flags, left, right).astype(BF16)
    to_far[0:192, :] = choose(flags, right, left).astype(BF16)
    narrow = lanes((96, 128))
    above = roll_lanes(from_upper[0:96, :].astype(F32), -80)
    middle = own_coarse[...]
    below = roll_lanes(from_lower[0:96, :].astype(F32), -80)
    for index, part in enumerate((above, middle, below)):
        coarse_strip[index * 96 : index * 96 + 96, :] = jnp.where(narrow < 40, part, 0.0)
    packed = jnp.where(narrow < 40, above, jnp.where(narrow < 80, roll_lanes(middle, 40), roll_lanes(below, 80)))
    to_near[192:288, :] = packed.astype(BF16)
    to_far[192:288, :] = packed.astype(BF16)


def pad_store(target, row, pooled, groups):
    rows = pooled.shape[0]
    place = lax.broadcasted_iota(jnp.int32, (SIDE, 128), 0)
    target[pl.ds(row + 1, rows), SIDE : SIDE + groups * SIDE, :] = pooled.reshape(
        rows, groups * SIDE, 128
    ).astype(BF16)
    for r in range(rows):
        before = pltpu.roll(pooled[r, groups - 1], 1, 0)
        after = pltpu.roll(pooled[r, 0], SIDE - 1, 0)
        target[row + 1 + r, 0:SIDE, :] = jnp.where(place == 0, 0.0, before).astype(BF16)
        target[row + 1 + r, SIDE + groups * SIDE : 2 * SIDE + groups * SIDE, :] = jnp.where(
            place == SIDE - 1, 0.0, after
        ).astype(BF16)


def halve(values, pairs, groups):
    summed = (values[:, 0:128] + values[:, 128:256]).reshape(pairs, groups // 2, 2, SIDE, 128)
    return 0.25 * (summed[:, :, 0] + summed[:, :, 1])


def norm_silu(values, mean_w):
    squares = dot_nn((values * values).astype(BF16), mean_w)
    half = values * lax.rsqrt(squares + 4.0 * epsilon)
    return half + half * jnp.tanh(half)


def conv_rows(source, weight, pair, pairs, groups):
    taps = [
        jnp.concatenate(
            [
                source[2 * (pair + m) + rr, dc * SIDE : dc * SIDE + groups * SIDE, :]
                for m in range(pairs)
            ],
            axis=0,
        )
        for rr in range(4)
        for dc in range(3)
    ]
    return dot_nn(jnp.concatenate(taps, axis=1), weight)


CORE_SCRATCH = [
    pltpu.VMEM((3, 400, 128), F32),
    pltpu.VMEM((PAIRS, 128, 256), BF16),
    pltpu.VMEM((50, 96, 128), BF16),
    pltpu.VMEM((26, 64, 128), BF16),
    pltpu.VMEM((14, 48, 128), BF16),
    pltpu.VMEM((24, 64, 256), F32),
    pltpu.VMEM((12, 32, 256), F32),
    pltpu.VMEM((3, 392, 128), F32),
    pltpu.VMEM((3, 400, 128), F32),
]


def denoise(state, cond_rows, weights, constants, scratch, noise_level, out):
    first_w, expand_w, project_w, level_w, last_level_w, final_w = weights
    shifts, back, mean_w, pool, grow = constants
    scaled, hidden, pooled1, pooled2, pooled3, level1, level2, taps_a, taps_b = scratch
    total_sq = noise_level * noise_level + sigma_data * sigma_data

    for shift in range(3):
        scaled[shift, 0:8, :] = jnp.zeros((8, 128), F32)
        scaled[shift, 384:400, :] = jnp.zeros((16, 128), F32)
        taps_a[shift, 384:392, :] = jnp.zeros((8, 128), F32)
        taps_b[shift, 0:8, :] = jnp.zeros((8, 128), F32)
    base = (state[...] * (1.0 / math.sqrt(total_sq))).astype(BF16)
    for shift in range(3):
        scaled[shift, 4 : 4 + ROWS, :] = dot_nn(base, shifts[:, shift * 128 : shift * 128 + 128])
    for buffer, rows in ((pooled1, 50), (pooled2, 26), (pooled3, 14)):
        blank = jnp.zeros(buffer.shape[1:], BF16)
        buffer[0] = blank
        buffer[rows - 1] = blank

    def first(c, carry):
        turned = []
        for k in range(FIRST_BATCH):
            row = pl.multiple_of(8 * FIRST_BATCH * c, 8) + 8 * k
            columns = [scaled[shift, pl.ds(row, 16), :].astype(BF16) for shift in range(3)]
            turned.append(jnp.concatenate(columns + [cond_rows[FIRST_BATCH * c + k]], axis=0).T)
        pre = dot_nn(jnp.concatenate(turned, axis=0), first_w[...])
        act = norm_silu(pre, mean_w[...])
        hidden[pl.ds(FIRST_BATCH * c, FIRST_BATCH)] = act.astype(BF16).reshape(FIRST_BATCH, 128, 256)
        summed = (act[:, 0:128] + act[:, 128:256]).reshape(FIRST_BATCH, 4, 2, SIDE, 128)
        pad_store(pooled1, FIRST_BATCH * c, 0.25 * (summed[:, :, 0] + summed[:, :, 1]), 4)
        return carry

    lax.fori_loop(0, PAIRS // FIRST_BATCH, first, 0)

    def one(c, carry):
        act = norm_silu(conv_rows(pooled1, level_w[0], LEVEL1_BATCH * c, LEVEL1_BATCH, 4), mean_w[...])
        level1[pl.ds(LEVEL1_BATCH * c, LEVEL1_BATCH)] = act.reshape(LEVEL1_BATCH, 64, 256)
        pad_store(pooled2, LEVEL1_BATCH * c, halve(act, LEVEL1_BATCH, 4), 2)
        return carry

    lax.fori_loop(0, 24 // LEVEL1_BATCH, one, 0)

    act = norm_silu(conv_rows(pooled2, level_w[1], 0, 12, 2), mean_w[...])
    level2[...] = act.reshape(12, 32, 256)
    pad_store(pooled3, 0, halve(act, 12, 2), 1)

    act3 = norm_silu(conv_rows(pooled3, level_w[2], 0, 6, 1), mean_w[...])
    act3 = jnp.concatenate([act3[:, 0:128], act3[:, 128:256]], axis=0)
    shifted = dot_nn(pool[...], act3.astype(BF16)).astype(BF16)
    act4 = norm_silu(
        dot_nn(jnp.concatenate([shifted[48 * k : 48 * k + 48] for k in range(9)], axis=1), last_level_w[...]),
        mean_w[0:128, 0:128],
    )
    merged3 = act3 + dot_nn(grow[...], act4.astype(BF16))
    for a in range(12):
        start = a % 2 * 96 + a // 2 * SIDE
        above = merged3[start : start + SIDE]
        above = jnp.concatenate([above, above], axis=0)
        level2[a] = level2[a] + jnp.concatenate([above, above], axis=1)

    def last(c, carry):
        merged = []
        for k in range(LAST_BATCH):
            half_of = slice(k % 2 * 128, k % 2 * 128 + 128)
            quarter_of = slice(k // 2 % 2 * 128, k // 2 % 2 * 128 + 128)
            coarse2 = level2[LAST_BATCH // 4 * c + k // 4, :, quarter_of].reshape(2, 1, SIDE, 128)
            merged1 = level1[LAST_BATCH // 2 * c + k // 2, :, half_of].reshape(2, 2, SIDE, 128) + coarse2
            merged1 = merged1.reshape(4, 1, SIDE, 128)
            merged1 = jnp.concatenate([merged1, merged1], axis=1).reshape(128, 128)
            merged.append(jnp.concatenate([merged1, merged1], axis=1))
        merged = jnp.concatenate(merged, axis=0)
        before = hidden[pl.ds(LAST_BATCH * c, LAST_BATCH)].reshape(LAST_BATCH * 128, 256)
        joined = (before.astype(F32) + merged).astype(BF16)
        half = dot_nn(joined, expand_w[...])
        inner = (half + half * jnp.tanh(half)).astype(BF16)
        mixed = (joined.astype(F32) + dot_nn(inner, project_w[...])).astype(BF16)
        for k in range(LAST_BATCH):
            taps = dot_nt(final_w[...], mixed[128 * k : 128 * k + 128])
            row = pl.multiple_of(8 * LAST_BATCH * c, 8) + 8 * k
            for shift in range(3):
                taps_a[shift, pl.ds(row, 8), :] = taps[16 * shift : 16 * shift + 8]
                taps_b[shift, pl.ds(row + 8, 8), :] = taps[16 * shift + 8 : 16 * shift + 16]
        return carry

    lax.fori_loop(0, PAIRS // LAST_BATCH, last, 0)

    parts = []
    for shift in range(3):
        total = taps_a[shift, 4 : 4 + ROWS, :] + taps_b[shift, 4 : 4 + ROWS, :]
        upper = total.astype(BF16)
        parts += [upper, (total - upper.astype(F32)).astype(BF16)]
    refined = dot_nn(jnp.concatenate(parts, axis=1), back[...])
    skip_scale = sigma_data * sigma_data / total_sq
    out_scale = noise_level * sigma_data / math.sqrt(total_sq)
    out[...] = skip_scale * state[...] + out_scale * refined


def inside_rows(flags):
    row = lax.broadcasted_iota(jnp.int32, (ROWS, 128), 0)
    outside = ((row < 4 * MARGIN) & (flags[0:1, :] < 0.25)) | (
        (row >= ROWS - 4 * MARGIN) & (flags[1:2, :] < 0.25)
    )
    return jnp.logical_not(outside)


def send_rows(flags, den, to_upper, to_lower, count):
    above, below = flags[0:1, :], flags[1:2, :]
    to_upper[...] = (above * den[0:count, :]).astype(BF16)
    to_lower[...] = (below * den[ROWS - count : ROWS, :]).astype(BF16)
    half = ROWS // 2
    den[0:half, :] = (1.0 - above) * den[0:half, :]
    den[half:ROWS, :] = (1.0 - below) * den[half:ROWS, :]


def first_kernel(
    row_map, row_frac, flags, col_map, col_frac, strip, coarse_strip, from_far, from_near,
    first_w, expand_w, project_w, level_w, last_level_w, final_w, shifts, back, mean_w, pool, grow,
    den, to_upper, to_lower, state, churn, cond_rows,
    window, coarse_t, *scratch,
):
    lat, lon = lax.axis_index("lat"), lax.axis_index("lon")
    lane = lanes((192, 128))
    inside = inside_rows(flags)
    near, far = from_near[...].astype(F32), from_far[...].astype(F32)
    from_left, from_right = choose(flags, near, far), choose(flags, far, near)
    for which, target in enumerate((state, churn)):
        for part in range(2):
            group = 2 * which + part
            rows = slice(part * 192, part * 192 + 192)
            left = roll_lanes(from_left[0:192, :], -32 * group)
            right = roll_lanes(from_right[0:192, :], 104 - 32 * group)
            target[rows, :] = jnp.where(lane < 24, left, jnp.where(lane < 104, strip[which, rows, :], right))
    state[...] = jnp.where(inside, level_first * state[...], 0.0)

    narrow = lanes((96, 128))
    for t, source in enumerate((from_left, None, from_right)):
        for part in range(3):
            if source is None:
                rows = coarse_strip[part * 96 : part * 96 + 96, :]
            else:
                rows = roll_lanes(source[192:288, :], -40 * part)
            for j in range(6):
                window[part * 6 + j, t * 16 : t * 16 + 16, :] = rows[j * 16 : j * 16 + 16]
    unit = jnp.where(
        lanes((40, 128)) == lax.broadcasted_iota(jnp.int32, (40, 128), 0), 1.0, 0.0
    ).astype(BF16)
    for j in range(18):
        coarse_t[j] = dot_nt(unit, window[j].astype(BF16))

    begin = lon * TILE_COLS - MARGIN
    begin = jnp.where(begin < 0, begin + 32 * TILE_COLS, begin)
    row, skip = begin // 128, begin % 128
    after = jnp.where(row == 19, 0, row + 1)
    turn = jnp.where(skip == 0, 0, 128 - skip)
    front = lanes((1, 128)) < 128 - skip

    def stretch(ref):
        return jnp.where(
            front, pltpu.roll(ref[pl.ds(row, 1), :], turn, 1), pltpu.roll(ref[pl.ds(after, 1), :], turn, 1)
        )

    offset = stretch(col_map) - (10 * lon - 10)
    offset = jnp.where(offset < 0, offset + 320, offset)
    offset = jnp.where(offset >= 320, offset - 320, offset)
    slot = lax.broadcasted_iota(jnp.int32, (COARSE_SLOTS, 128), 0)
    tile = jnp.where(slot >= 32, 2, jnp.where(slot >= 16, 1, 0))
    column = jnp.where(slot - 16 * tile < 10, slot - 6 * tile, -1)
    fraction = stretch(col_frac)
    mix = jnp.where(column == offset, 1.0 - fraction, 0.0) + jnp.where(column == offset + 1, fraction, 0.0)
    mix = dot_nn(mix.astype(BF16), shifts[:, 128:256]).astype(BF16)

    def coarse_row(p):
        y = lat * TILE_ROWS - MARGIN + p
        within = (y >= 0) & (y < 8 * TILE_ROWS)
        y = jnp.clip(y, 0, 8 * TILE_ROWS - 1)
        at = jnp.clip(row_map[y] - (lat * 6 - 6), 0, 16)
        weight = row_frac[y]
        near = jnp.where(within, 1.0 - weight, 0.0)
        far = jnp.where(within, weight, 0.0)
        return near * coarse_t[at] + far * coarse_t[at + 1]

    def interpolate(c, carry):
        rows = [coarse_row(2 * COND_BATCH * c + k) for k in range(2 * COND_BATCH)]
        fine = dot_nn(jnp.concatenate(rows, axis=0).astype(BF16), mix)
        cond_rows[pl.ds(COND_BATCH * c, COND_BATCH)] = fine.astype(BF16).reshape(COND_BATCH, 80, 128)
        return carry

    lax.fori_loop(0, PAIRS // COND_BATCH, interpolate, 0)

    denoise(
        state, cond_rows, (first_w, expand_w, project_w, level_w, last_level_w, final_w),
        (shifts, back, mean_w, pool, grow), scratch, level_first, den,
    )
    send_rows(flags, den, to_upper, to_lower, 192)


def add_rows_kernel(flags, den, from_upper, from_lower, total, to_far, to_near):
    top = den[0:192, :] + from_upper[...].astype(F32)
    bottom = den[192:384, :] + from_lower[...].astype(F32)
    total[0:192, :] = top
    total[192:384, :] = bottom
    lane = lanes((192, 128))
    left = jnp.where(lane < 64, top, roll_lanes(bottom, 64))
    right = jnp.where(lane < 64, roll_lanes(top, -80), roll_lanes(bottom, 64 - 80))
    to_near[...] = choose(flags, left, right).astype(BF16)
    to_far[...] = choose(flags, right, left).astype(BF16)


def second_kernel(
    flags, total, from_far, from_near, state, churn, cond_rows,
    first_w, expand_w, project_w, level_w, last_level_w, final_w, shifts, back, mean_w, pool, grow,
    den, to_upper, to_lower, raised,
    *scratch,
):
    lane = lanes((192, 128))
    edge = (lane < 48) | (lane >= 80)
    near, far = from_near[...].astype(F32), from_far[...].astype(F32)
    left, right = choose(flags, near, far), choose(flags, far, near)
    inside = inside_rows(flags)
    for part in range(2):
        rows = slice(part * 192, part * 192 + 192)
        from_l = roll_lanes(left, -64 * part)
        from_r = roll_lanes(right, 80 - 64 * part)
        summed = total[rows, :] + jnp.where(lane < 48, from_l, jnp.where(lane >= 80, from_r, 0.0))
        blended = summed * jnp.where(edge, 0.5, 1.0)
        value = state[rows, :]
        value = value + (level_second - level_first) / level_first * (value - blended)
        value = value + math.sqrt(level_raised * level_raised - level_second * level_second) * churn[rows, :]
        raised[rows, :] = value
    raised[...] = jnp.where(inside, raised[...], 0.0)
    denoise(
        raised, cond_rows, (first_w, expand_w, project_w, level_w, last_level_w, final_w),
        (shifts, back, mean_w, pool, grow), scratch, level_raised, den,
    )
    send_rows(flags, den, to_upper, to_lower, 96)


def add_tile_rows_kernel(flags, den, from_upper, from_lower, total, to_far, to_near):
    top = den[96:192, :] + from_upper[...].astype(F32)
    bottom = den[192:288, :] + from_lower[...].astype(F32)
    total[0:96, :] = top
    total[96:192, :] = bottom
    lane = lanes((96, 128))
    left = jnp.where(lane < 64, top, roll_lanes(bottom, 64))
    right = jnp.where(lane < 64, roll_lanes(top, -104), roll_lanes(bottom, 64 - 104))
    to_near[...] = choose(flags, left, right).astype(BF16)
    to_far[...] = choose(flags, right, left).astype(BF16)


def finish_kernel(flags, total, from_far, from_near, raised, out, rows_ref):
    lane = lanes((96, 128))
    edge = (lane < 48) | (lane >= 80)
    near, far = from_near[...].astype(F32), from_far[...].astype(F32)
    left, right = choose(flags, near, far), choose(flags, far, near)
    for part in range(2):
        rows = slice(part * 96, part * 96 + 96)
        from_l = roll_lanes(left, 24 - 64 * part)
        from_r = roll_lanes(right, 80 - 64 * part)
        use_l = (lane >= 24) & (lane < 48)
        use_r = (lane >= 80) & (lane < 104)
        summed = total[rows, :] + jnp.where(use_l, from_l, jnp.where(use_r, from_r, 0.0))
        blended = summed * jnp.where(edge, 0.5, 1.0)
        value = raised[96 + part * 96 : 192 + part * 96, :]
        value = value + (level_final - level_raised) / level_raised * (value - blended)
        rows_ref[rows, :] = roll_lanes(value, -24)
    for e in range(4):
        out[e] = rows_ref[pl.ds(e, TILE_ROWS, stride=4), 0:TILE_COLS]


def shape(dims, dtype):
    return jax.ShapeDtypeStruct(dims, dtype)


def call(kernel, operands, outs, scratch=(), scalars=0, cost=(0, 0, 0), far=()):
    operands = [
        pltpu.with_memory_space_constraint(a, pltpu.HBM) if n in far else a for n, a in enumerate(operands)
    ]
    return pl.pallas_call(
        kernel,
        out_shape=outs,
        in_specs=[pl.BlockSpec(memory_space=pltpu.SMEM)] * scalars
        + [pl.BlockSpec(memory_space=pltpu.VMEM)] * (len(operands) - scalars),
        out_specs=[pl.BlockSpec(memory_space=pltpu.VMEM)] * len(outs),
        scratch_shapes=list(scratch),
        compiler_params=pltpu.CompilerParams(vmem_limit_bytes=40 << 20),
        cost_estimate=pl.CostEstimate(flops=cost[0], bytes_accessed=cost[1], transcendentals=cost[2]),
    )(*operands)


def body(
    coarse, row_map, row_frac, col_map, col_frac, noise_init, noise_churn,
    w_state, w_cond, w_expand, w_project, w_levels, w_final,
):
    lats, lons = lax.axis_size("lat"), lax.axis_size("lon")
    up = [(i, (i + 1) % lats) for i in range(lats)]
    down = [((i + 1) % lats, i) for i in range(lats)]
    near = [(i, i ^ 1) for i in range(lons)]
    far = [(i, (i + 2 * (i % 2) - 1) % lons) for i in range(lons)]

    def swap_rows(to_upper, to_lower):
        return lax.ppermute(to_lower, "lat", up), lax.ppermute(to_upper, "lat", down)

    def swap_cols(to_near, to_far):
        from_far = lax.ppermute(to_far, "lon", far)
        return from_far, lax.ppermute(to_near, "lon", near)

    msg = shape((192, 128), BF16)
    to_upper, to_lower, own, own_coarse = call(
        pack_rows_kernel,
        (noise_init, noise_churn, coarse.transpose(2, 1, 0)),
        [msg, msg, shape((2, 192, 128), F32), shape((96, 128), F32)],
        [pltpu.VMEM((2, 192, 128), F32)],
        far=(0, 1, 2),
    )
    from_upper, from_lower = swap_rows(to_upper, to_lower)
    mean_w = np.zeros((256, 256), np.float32)
    mean_w[:128, :128] = mean_w[128:, 128:] = 4.0 / 128.0
    constants = [jnp.asarray(c, BF16) for c in (SHIFTS, BACK, mean_w, POOL, GROW)]
    prepared = call(
        prepare_kernel,
        (
            w_state.T, w_cond.T, w_expand, w_project, w_levels, w_final, jnp.asarray(PICKS, BF16), *constants, col_map.reshape(20, 128), col_frac.reshape(20, 128),
        ),
        [
            shape((128, 256), BF16), shape((256, 256), BF16), shape((256, 256), BF16),
            shape((3, 1536, 256), BF16), shape((1152, 128), BF16), shape((48, 256), BF16),
            *[shape(c.shape, BF16) for c in constants],
            shape((20, 128), jnp.int32), shape((20, 128), F32), shape((8, 128), F32),
        ],
        [pltpu.VMEM((36, 128), F32)],
        cost=(2 * 36 * 128**3, 4 << 20, 0),
        far=range(14),
    )
    weights, constants, (col_map, col_frac, flags) = prepared[:6], prepared[6:11], prepared[11:]
    wide_msg = shape((288, 128), BF16)
    to_far, to_near, strip, coarse_strip = call(
        pack_cols_kernel,
        (flags, from_upper, from_lower, own, own_coarse),
        [wide_msg, wide_msg, shape((2, ROWS, 128), F32), shape((288, 128), F32)],
    )
    from_far, from_near = swap_cols(to_near, to_far)

    field = shape((ROWS, 128), F32)
    cost = (5 * 10**9, 8 << 20, 3 * 10**6)
    den, to_upper, to_lower, state, churn, cond_rows = call(
        first_kernel,
        (
            row_map, row_frac, flags, col_map, col_frac,
            strip, coarse_strip, from_far, from_near, *weights, *constants,
        ),
        [
            field, msg, msg, field, field,
            shape((PAIRS, 80, 128), BF16),
        ],
        [pltpu.VMEM((18, COARSE_SLOTS, 128), F32), pltpu.VMEM((18, 40, COARSE_SLOTS), F32)] + CORE_SCRATCH,
        scalars=2,
        cost=cost,
        far=(0, 1),
    )
    from_upper, from_lower = swap_rows(to_upper, to_lower)
    total, to_far, to_near = call(
        add_rows_kernel, (flags, den, from_upper, from_lower), [field, msg, msg]
    )
    from_far, from_near = swap_cols(to_near, to_far)
    short_msg = shape((96, 128), BF16)
    den, to_upper, to_lower, raised = call(
        second_kernel,
        (
            flags, total, from_far, from_near, state, churn, cond_rows,
            *weights, *constants,
        ),
        [field, short_msg, short_msg, field],
        CORE_SCRATCH,
        cost=cost,
    )
    from_upper, from_lower = swap_rows(to_upper, to_lower)
    total, to_far, to_near = call(
        add_tile_rows_kernel,
        (flags, den, from_upper, from_lower),
        [shape((192, 128), F32), short_msg, short_msg],
    )
    from_far, from_near = swap_cols(to_near, to_far)
    (final,) = call(
        finish_kernel,
        (flags, total, from_far, from_near, raised),
        [shape((4, TILE_ROWS, TILE_COLS), F32)],
        [pltpu.VMEM((192, 128), F32)],
    )
    return final


def solution(mesh):
    sharded = P(None, "lat", "lon")
    return jax.shard_map(
        body,
        mesh=mesh,
        in_specs=(sharded, P(), P(), P(), P(), sharded, sharded) + (P(),) * 6,
        out_specs=sharded,
        check_vma=False,
    )
```

```python
import math

import jax
import jax.numpy as jnp
import numpy as np
from jax import lax
from jax.experimental import pallas as pl
from jax.experimental.pallas import tpu as pltpu
from jax.sharding import PartitionSpec as P

MARGIN = 24
TILE_ROWS, TILE_COLS = 48, 80
PATCH_ROWS, PATCH_COLS = 96, 128
CH = 128
ROWS = 4 * PATCH_ROWS
PAIRS = PATCH_ROWS // 2
FIRST_BATCH, LAST_BATCH = 16, 48
LEVEL1_BATCH, COND_BATCH = 12, 24
SIDE = 16
COARSE_SLOTS = 48

sigma_data = 0.5
level_first = 4.0
level_second = 1.0
level_raised = 1.5
level_final = 0.25
epsilon = 1e-06

F32 = jnp.float32
BF16 = jnp.bfloat16


def _constants():
    place = np.arange(128)
    column = 8 * (place % 16) + place // 16
    shifts = [
        (np.arange(128)[:, None] == (column + shift - 1)[None, :]).astype(np.float32) for shift in range(3)
    ]
    shifts = np.concatenate(shifts, 1)
    back = []
    for shift in range(3):
        one = (column[:, None] == (np.arange(128) + shift - 1)[None, :]).astype(np.float32)
        back += [one, one]
    back = np.concatenate(back, 0)
    pick_in = np.zeros((2, 48, 128), np.float32)
    pick_out = np.zeros((2, 48, 128), np.float32)
    pick_cond = np.zeros((2, 80, 128), np.float32)
    for pi in range(2):
        pick_cond[pi, pi * 40 + np.arange(40), np.arange(40)] = 1.0
        for dc in range(3):
            for pp in range(4):
                for e in range(4):
                    dr = pp - pi
                    if 0 <= dr <= 2:
                        pick_in[pi, dc * 16 + pp * 4 + e, (3 * dr + dc) * 4 + e] = 1.0
                    dr = pi + 2 - pp
                    if 0 <= dr <= 2:
                        pick_out[pi, dc * 16 + pp * 4 + e, (3 * dr + dc) * 4 + e] = 1.0
    picks = np.concatenate([v.reshape(-1, 128) for v in (pick_in, pick_cond, pick_out, np.eye(128))], 0)
    pool = np.zeros((9, 6, 8, 12, 16), np.float32)
    for dr in range(3):
        for dc in range(3):
            for r in range(6):
                for c in range(8):
                    rr, cc = r + dr - 1, c + dc - 1
                    if 0 <= rr < 6 and 0 <= cc < 8:
                        pool[3 * dr + dc, r, c, 2 * rr : 2 * rr + 2, 2 * cc : 2 * cc + 2] = 0.25
    pool = pool.reshape(432, 6, 2, 16).transpose(0, 2, 1, 3).reshape(432, 192)
    grow = np.zeros((12, 16, 6, 8), np.float32)
    for r in range(12):
        for c in range(16):
            grow[r, c, r // 2, c // 2] = 1.0
    grow = grow.reshape(6, 2, 16, 48).transpose(1, 0, 2, 3).reshape(192, 48)
    return shifts, back, picks, pool, grow


SHIFTS, BACK, PICKS, POOL, GROW = _constants()


def dot_nt(a, b):
    return lax.dot_general(a, b, (((1,), (1,)), ((), ())), preferred_element_type=F32)


def dot_nn(a, b):
    return jnp.dot(a, b, preferred_element_type=F32)


def lanes(shape):
    return lax.broadcasted_iota(jnp.int32, shape, 1)


def choose(flags, first, second):
    return jnp.where(flags[2:3, :] > 0.5, first, second)


def roll_lanes(value, amount):
    amount = amount % 128
    return value if amount == 0 else pltpu.roll(value, amount, 1)


def prepare_kernel(
    w_state, w_cond, w_expand, w_project, w_levels, w_final, picks, shifts, back, mean_w, pool, grow, col_map, col_frac,
    first_w, expand_w, project_w, level_w, last_level_w, final_w,
    own_shifts, own_back, own_mean_w, own_pool, own_grow, own_col_map, own_col_frac, flags, flat_final,
):
    for source, target in (
        (shifts, own_shifts), (back, own_back), (mean_w, own_mean_w), (pool, own_pool), (grow, own_grow),
        (col_map, own_col_map), (col_frac, own_col_frac),
    ):
        target[...] = source[...]
    lat, lon = lax.axis_index("lat"), lax.axis_index("lon")
    row = lax.broadcasted_iota(jnp.int32, (8, 128), 0)
    above = jnp.where(lat > 0, 0.5, 0.0)
    below = jnp.where(lat < 7, 0.5, 0.0)
    odd = jnp.where(lon % 2 == 1, 1.0, 0.0)
    flags[...] = jnp.where(row == 0, above, jnp.where(row == 1, below, odd))
    unit = picks[352:480, :]
    for k in range(9):
        flat_final[4 * k : 4 * k + 4, :] = w_final[k].astype(F32)
    final_rows = flat_final[...].astype(BF16)
    for pi in range(2):
        part = slice(pi * 128, pi * 128 + 128)
        first_w[0:48, part] = dot_nn(picks[pi * 48 : pi * 48 + 48, 0:36], w_state[...]).astype(BF16)
        first_w[48:128, part] = dot_nn(picks[96 + pi * 80 : 176 + pi * 80, 0:40], w_cond[...]).astype(BF16)
        final_w[:, part] = dot_nn(picks[256 + pi * 48 : 304 + pi * 48, 0:36], final_rows).astype(BF16)
    zero = jnp.zeros((128, 128), BF16)
    for source, target, factor in ((w_expand, expand_w, 0.5), (w_project, project_w, 1.0)):
        block = (dot_nt(unit, source[...]) * factor).astype(BF16)
        target[0:128, 0:128] = block
        target[128:256, 128:256] = block
        target[0:128, 128:256] = zero
        target[128:256, 0:128] = zero
    for level in range(3):
        for dc in range(3):
            level_w[level, (9 + dc) * 128 : (10 + dc) * 128, 0:128] = zero
            level_w[level, dc * 128 : dc * 128 + 128, 128:256] = zero
            for dr in range(3):
                block = dot_nt(unit, w_levels[level, 3 * dr + dc]).astype(BF16)
                for pi in range(2):
                    start = (3 * (dr + pi) + dc) * 128
                    level_w[level, start : start + 128, pi * 128 : pi * 128 + 128] = block
    for k in range(9):
        last_level_w[k * 128 : k * 128 + 128, :] = dot_nt(unit, w_levels[3, k]).astype(BF16)


def pack_rows_kernel(noise_init, noise_churn, coarse, to_upper, to_lower, own, own_coarse, padded):
    for which, noise in enumerate((noise_init, noise_churn)):
        for e in range(4):
            padded[which, pl.ds(e, TILE_ROWS, stride=4), 0:TILE_COLS] = noise[e]
    own_coarse[...] = jnp.zeros((96, 128), F32)
    for k in range(10):
        own_coarse[pl.ds(k, 6, stride=16), 0:40] = coarse[k].astype(F32)
    lane = lanes((96, 128))
    placed = roll_lanes(own_coarse[...], 80)
    for which in range(2):
        own[which] = padded[which]
        for target, start in ((to_upper, 0), (to_lower, 96)):
            part = padded[which, start : start + 96, :]
            if which == 0:
                part = jnp.where(lane < 80, part, placed)
            target[which * 96 : which * 96 + 96, :] = part.astype(BF16)


def pack_cols_kernel(flags, from_upper, from_lower, own, own_coarse, to_far, to_near, strip, coarse_strip):
    lane = lanes((192, 128))
    for which in range(2):
        rows = slice(which * 96, which * 96 + 96)
        strip[which, 0:96, :] = roll_lanes(from_upper[rows, :].astype(F32), MARGIN)
        strip[which, 96:288, :] = roll_lanes(own[which], MARGIN)
        strip[which, 288:384, :] = roll_lanes(from_lower[rows, :].astype(F32), MARGIN)
    left = right = None
    for group in range(4):
        part = strip[group // 2, (group % 2) * 192 : (group % 2) * 192 + 192, :]
        for_left = roll_lanes(part, 32 * group - 24)
        for_right = roll_lanes(part, 32 * group - 80)
        inside = (lane >= 32 * group) & (lane < 32 * group + 32)
        left = for_left if group == 0 else jnp.where(inside, for_left, left)
        right = for_right if group == 0 else jnp.where(inside, for_right, right)
    to_near[0:192, :] = choose(flags, left, right).astype(BF16)
    to_far[0:192, :] = choose(flags, right, left).astype(BF16)
    narrow = lanes((96, 128))
    above = roll_lanes(from_upper[0:96, :].astype(F32), -80)
    middle = own_coarse[...]
    below = roll_lanes(from_lower[0:96, :].astype(F32), -80)
    for index, part in enumerate((above, middle, below)):
        coarse_strip[index * 96 : index * 96 + 96, :] = jnp.where(narrow < 40, part, 0.0)
    packed = jnp.where(narrow < 40, above, jnp.where(narrow < 80, roll_lanes(middle, 40), roll_lanes(below, 80)))
    to_near[192:288, :] = packed.astype(BF16)
    to_far[192:288, :] = packed.astype(BF16)


def pad_store(target, row, pooled, groups):
    rows = pooled.shape[0]
    place = lax.broadcasted_iota(jnp.int32, (SIDE, 128), 0)
    target[pl.ds(row + 1, rows), SIDE : SIDE + groups * SIDE, :] = pooled.reshape(
        rows, groups * SIDE, 128
    ).astype(BF16)
    for r in range(rows):
        before = pltpu.roll(pooled[r, groups - 1], 1, 0)
        after = pltpu.roll(pooled[r, 0], SIDE - 1, 0)
        target[row + 1 + r, 0:SIDE, :] = jnp.where(place == 0, 0.0, before).astype(BF16)
        target[row + 1 + r, SIDE + groups * SIDE : 2 * SIDE + groups * SIDE, :] = jnp.where(
            place == SIDE - 1, 0.0, after
        ).astype(BF16)


def halve(values, pairs, groups):
    summed = (values[:, 0:128] + values[:, 128:256]).reshape(pairs, groups // 2, 2, SIDE, 128)
    return 0.25 * (summed[:, :, 0] + summed[:, :, 1])


def norm_silu(values, mean_w):
    squares = dot_nn((values * values).astype(BF16), mean_w)
    half = values * lax.rsqrt(squares + 4.0 * epsilon)
    return half + half * jnp.tanh(half)


def conv_rows(source, weight, pair, pairs, groups):
    taps = [
        jnp.concatenate(
            [
                source[2 * (pair + m) + rr, dc * SIDE : dc * SIDE + groups * SIDE, :]
                for m in range(pairs)
            ],
            axis=0,
        )
        for rr in range(4)
        for dc in range(3)
    ]
    return dot_nn(jnp.concatenate(taps, axis=1), weight)


CORE_SCRATCH = [
    pltpu.VMEM((3, 400, 128), F32),
    pltpu.VMEM((PAIRS, 128, 256), BF16),
    pltpu.VMEM((50, 96, 128), BF16),
    pltpu.VMEM((26, 64, 128), BF16),
    pltpu.VMEM((14, 48, 128), BF16),
    pltpu.VMEM((24, 64, 256), F32),
    pltpu.VMEM((12, 32, 256), F32),
    pltpu.VMEM((3, 392, 128), F32),
    pltpu.VMEM((3, 400, 128), F32),
]


def denoise(state, cond_rows, weights, constants, scratch, noise_level, out):
    first_w, expand_w, project_w, level_w, last_level_w, final_w = weights
    shifts, back, mean_w, pool, grow = constants
    scaled, hidden, pooled1, pooled2, pooled3, level1, level2, taps_a, taps_b = scratch
    total_sq = noise_level * noise_level + sigma_data * sigma_data

    for shift in range(3):
        scaled[shift, 0:8, :] = jnp.zeros((8, 128), F32)
        scaled[shift, 384:400, :] = jnp.zeros((16, 128), F32)
        taps_a[shift, 384:392, :] = jnp.zeros((8, 128), F32)
        taps_b[shift, 0:8, :] = jnp.zeros((8, 128), F32)
    base = (state[...] * (1.0 / math.sqrt(total_sq))).astype(BF16)
    for shift in range(3):
        scaled[shift, 4 : 4 + ROWS, :] = dot_nn(base, shifts[:, shift * 128 : shift * 128 + 128])
    for buffer, rows in ((pooled1, 50), (pooled2, 26), (pooled3, 14)):
        blank = jnp.zeros(buffer.shape[1:], BF16)
        buffer[0] = blank
        buffer[rows - 1] = blank

    def first(c, carry):
        turned = []
        for k in range(FIRST_BATCH):
            row = pl.multiple_of(8 * FIRST_BATCH * c, 8) + 8 * k
            columns = [scaled[shift, pl.ds(row, 16), :].astype(BF16) for shift in range(3)]
            turned.append(jnp.concatenate(columns + [cond_rows[FIRST_BATCH * c + k]], axis=0).T)
        pre = dot_nn(jnp.concatenate(turned, axis=0), first_w[...])
        act = norm_silu(pre, mean_w[...])
        hidden[pl.ds(FIRST_BATCH * c, FIRST_BATCH)] = act.astype(BF16).reshape(FIRST_BATCH, 128, 256)
        summed = (act[:, 0:128] + act[:, 128:256]).reshape(FIRST_BATCH, 4, 2, SIDE, 128)
        pad_store(pooled1, FIRST_BATCH * c, 0.25 * (summed[:, :, 0] + summed[:, :, 1]), 4)
        return carry

    lax.fori_loop(0, PAIRS // FIRST_BATCH, first, 0, unroll=True)

    def one(c, carry):
        act = norm_silu(conv_rows(pooled1, level_w[0], LEVEL1_BATCH * c, LEVEL1_BATCH, 4), mean_w[...])
        level1[pl.ds(LEVEL1_BATCH * c, LEVEL1_BATCH)] = act.reshape(LEVEL1_BATCH, 64, 256)
        pad_store(pooled2, LEVEL1_BATCH * c, halve(act, LEVEL1_BATCH, 4), 2)
        return carry

    lax.fori_loop(0, 24 // LEVEL1_BATCH, one, 0, unroll=True)

    act = norm_silu(conv_rows(pooled2, level_w[1], 0, 12, 2), mean_w[...])
    level2[...] = act.reshape(12, 32, 256)
    pad_store(pooled3, 0, halve(act, 12, 2), 1)

    act3 = norm_silu(conv_rows(pooled3, level_w[2], 0, 6, 1), mean_w[...])
    act3 = jnp.concatenate([act3[:, 0:128], act3[:, 128:256]], axis=0)
    shifted = dot_nn(pool[...], act3.astype(BF16)).astype(BF16)
    act4 = norm_silu(
        dot_nn(jnp.concatenate([shifted[48 * k : 48 * k + 48] for k in range(9)], axis=1), last_level_w[...]),
        mean_w[0:128, 0:128],
    )
    merged3 = act3 + dot_nn(grow[...], act4.astype(BF16))
    for a in range(12):
        start = a % 2 * 96 + a // 2 * SIDE
        above = merged3[start : start + SIDE]
        above = jnp.concatenate([above, above], axis=0)
        level2[a] = level2[a] + jnp.concatenate([above, above], axis=1)

    def last(c, carry):
        merged = []
        for k in range(LAST_BATCH):
            half_of = slice(k % 2 * 128, k % 2 * 128 + 128)
            quarter_of = slice(k // 2 % 2 * 128, k // 2 % 2 * 128 + 128)
            coarse2 = level2[LAST_BATCH // 4 * c + k // 4, :, quarter_of].reshape(2, 1, SIDE, 128)
            merged1 = level1[LAST_BATCH // 2 * c + k // 2, :, half_of].reshape(2, 2, SIDE, 128) + coarse2
            merged1 = merged1.reshape(4, 1, SIDE, 128)
            merged1 = jnp.concatenate([merged1, merged1], axis=1).reshape(128, 128)
            merged.append(jnp.concatenate([merged1, merged1], axis=1))
        merged = jnp.concatenate(merged, axis=0)
        before = hidden[pl.ds(LAST_BATCH * c, LAST_BATCH)].reshape(LAST_BATCH * 128, 256)
        joined = (before.astype(F32) + merged).astype(BF16)
        half = dot_nn(joined, expand_w[...])
        inner = (half + half * jnp.tanh(half)).astype(BF16)
        mixed = (joined.astype(F32) + dot_nn(inner, project_w[...])).astype(BF16)
        for k in range(LAST_BATCH):
            taps = dot_nt(final_w[...], mixed[128 * k : 128 * k + 128])
            row = pl.multiple_of(8 * LAST_BATCH * c, 8) + 8 * k
            for shift in range(3):
                taps_a[shift, pl.ds(row, 8), :] = taps[16 * shift : 16 * shift + 8]
                taps_b[shift, pl.ds(row + 8, 8), :] = taps[16 * shift + 8 : 16 * shift + 16]
        return carry

    lax.fori_loop(0, PAIRS // LAST_BATCH, last, 0)

    parts = []
    for shift in range(3):
        total = taps_a[shift, 4 : 4 + ROWS, :] + taps_b[shift, 4 : 4 + ROWS, :]
        upper = total.astype(BF16)
        parts += [upper, (total - upper.astype(F32)).astype(BF16)]
    refined = dot_nn(jnp.concatenate(parts, axis=1), back[...])
    skip_scale = sigma_data * sigma_data / total_sq
    out_scale = noise_level * sigma_data / math.sqrt(total_sq)
    out[...] = skip_scale * state[...] + out_scale * refined


def inside_rows(flags):
    row = lax.broadcasted_iota(jnp.int32, (ROWS, 128), 0)
    outside = ((row < 4 * MARGIN) & (flags[0:1, :] < 0.25)) | (
        (row >= ROWS - 4 * MARGIN) & (flags[1:2, :] < 0.25)
    )
    return jnp.logical_not(outside)


def send_rows(flags, den, to_upper, to_lower, count):
    above, below = flags[0:1, :], flags[1:2, :]
    to_upper[...] = (above * den[0:count, :]).astype(BF16)
    to_lower[...] = (below * den[ROWS - count : ROWS, :]).astype(BF16)
    half = ROWS // 2
    den[0:half, :] = (1.0 - above) * den[0:half, :]
    den[half:ROWS, :] = (1.0 - below) * den[half:ROWS, :]


def first_kernel(
    row_map, row_frac, flags, col_map, col_frac, strip, coarse_strip, from_far, from_near,
    first_w, expand_w, project_w, level_w, last_level_w, final_w, shifts, back, mean_w, pool, grow,
    den, to_upper, to_lower, state, churn, cond_rows,
    window, coarse_t, *scratch,
):
    lat, lon = lax.axis_index("lat"), lax.axis_index("lon")
    lane = lanes((192, 128))
    inside = inside_rows(flags)
    near, far = from_near[...].astype(F32), from_far[...].astype(F32)
    from_left, from_right = choose(flags, near, far), choose(flags, far, near)
    for which, target in enumerate((state, churn)):
        for part in range(2):
            group = 2 * which + part
            rows = slice(part * 192, part * 192 + 192)
            left = roll_lanes(from_left[0:192, :], -32 * group)
            right = roll_lanes(from_right[0:192, :], 104 - 32 * group)
            target[rows, :] = jnp.where(lane < 24, left, jnp.where(lane < 104, strip[which, rows, :], right))
    state[...] = jnp.where(inside, level_first * state[...], 0.0)

    narrow = lanes((96, 128))
    for t, source in enumerate((from_left, None, from_right)):
        for part in range(3):
            if source is None:
                rows = coarse_strip[part * 96 : part * 96 + 96, :]
            else:
                rows = roll_lanes(source[192:288, :], -40 * part)
            for j in range(6):
                window[part * 6 + j, t * 16 : t * 16 + 16, :] = rows[j * 16 : j * 16 + 16]
    unit = jnp.where(
        lanes((40, 128)) == lax.broadcasted_iota(jnp.int32, (40, 128), 0), 1.0, 0.0
    ).astype(BF16)
    for j in range(18):
        coarse_t[j] = dot_nt(unit, window[j].astype(BF16))

    begin = lon * TILE_COLS - MARGIN
    begin = jnp.where(begin < 0, begin + 32 * TILE_COLS, begin)
    row, skip = begin // 128, begin % 128
    after = jnp.where(row == 19, 0, row + 1)
    turn = jnp.where(skip == 0, 0, 128 - skip)
    front = lanes((1, 128)) < 128 - skip

    def stretch(ref):
        return jnp.where(
            front, pltpu.roll(ref[pl.ds(row, 1), :], turn, 1), pltpu.roll(ref[pl.ds(after, 1), :], turn, 1)
        )

    offset = stretch(col_map) - (10 * lon - 10)
    offset = jnp.where(offset < 0, offset + 320, offset)
    offset = jnp.where(offset >= 320, offset - 320, offset)
    slot = lax.broadcasted_iota(jnp.int32, (COARSE_SLOTS, 128), 0)
    tile = jnp.where(slot >= 32, 2, jnp.where(slot >= 16, 1, 0))
    column = jnp.where(slot - 16 * tile < 10, slot - 6 * tile, -1)
    fraction = stretch(col_frac)
    mix = jnp.where(column == offset, 1.0 - fraction, 0.0) + jnp.where(column == offset + 1, fraction, 0.0)
    mix = dot_nn(mix.astype(BF16), shifts[:, 128:256]).astype(BF16)

    def coarse_row(p):
        y = lat * TILE_ROWS - MARGIN + p
        within = (y >= 0) & (y < 8 * TILE_ROWS)
        y = jnp.clip(y, 0, 8 * TILE_ROWS - 1)
        at = jnp.clip(row_map[y] - (lat * 6 - 6), 0, 16)
        weight = row_frac[y]
        near = jnp.where(within, 1.0 - weight, 0.0)
        far = jnp.where(within, weight, 0.0)
        return near * coarse_t[at] + far * coarse_t[at + 1]

    def interpolate(c, carry):
        rows = [coarse_row(2 * COND_BATCH * c + k) for k in range(2 * COND_BATCH)]
        fine = dot_nn(jnp.concatenate(rows, axis=0).astype(BF16), mix)
        cond_rows[pl.ds(COND_BATCH * c, COND_BATCH)] = fine.astype(BF16).reshape(COND_BATCH, 80, 128)
        return carry

    lax.fori_loop(0, PAIRS // COND_BATCH, interpolate, 0)

    denoise(
        state, cond_rows, (first_w, expand_w, project_w, level_w, last_level_w, final_w),
        (shifts, back, mean_w, pool, grow), scratch, level_first, den,
    )
    send_rows(flags, den, to_upper, to_lower, 192)


def add_rows_kernel(flags, den, from_upper, from_lower, total, to_far, to_near):
    top = den[0:192, :] + from_upper[...].astype(F32)
    bottom = den[192:384, :] + from_lower[...].astype(F32)
    total[0:192, :] = top
    total[192:384, :] = bottom
    lane = lanes((192, 128))
    left = jnp.where(lane < 64, top, roll_lanes(bottom, 64))
    right = jnp.where(lane < 64, roll_lanes(top, -80), roll_lanes(bottom, 64 - 80))
    to_near[...] = choose(flags, left, right).astype(BF16)
    to_far[...] = choose(flags, right, left).astype(BF16)


def second_kernel(
    flags, total, from_far, from_near, state, churn, cond_rows,
    first_w, expand_w, project_w, level_w, last_level_w, final_w, shifts, back, mean_w, pool, grow,
    den, to_upper, to_lower, raised,
    *scratch,
):
    lane = lanes((192, 128))
    edge = (lane < 48) | (lane >= 80)
    near, far = from_near[...].astype(F32), from_far[...].astype(F32)
    left, right = choose(flags, near, far), choose(flags, far, near)
    inside = inside_rows(flags)
    for part in range(2):
        rows = slice(part * 192, part * 192 + 192)
        from_l = roll_lanes(left, -64 * part)
        from_r = roll_lanes(right, 80 - 64 * part)
        summed = total[rows, :] + jnp.where(lane < 48, from_l, jnp.where(lane >= 80, from_r, 0.0))
        blended = summed * jnp.where(edge, 0.5, 1.0)
        value = state[rows, :]
        value = value + (level_second - level_first) / level_first * (value - blended)
        value = value + math.sqrt(level_raised * level_raised - level_second * level_second) * churn[rows, :]
        raised[rows, :] = value
    raised[...] = jnp.where(inside, raised[...], 0.0)
    denoise(
        raised, cond_rows, (first_w, expand_w, project_w, level_w, last_level_w, final_w),
        (shifts, back, mean_w, pool, grow), scratch, level_raised, den,
    )
    send_rows(flags, den, to_upper, to_lower, 96)


def add_tile_rows_kernel(flags, den, from_upper, from_lower, total, to_far, to_near):
    top = den[96:192, :] + from_upper[...].astype(F32)
    bottom = den[192:288, :] + from_lower[...].astype(F32)
    total[0:96, :] = top
    total[96:192, :] = bottom
    lane = lanes((96, 128))
    left = jnp.where(lane < 64, top, roll_lanes(bottom, 64))
    right = jnp.where(lane < 64, roll_lanes(top, -104), roll_lanes(bottom, 64 - 104))
    to_near[...] = choose(flags, left, right).astype(BF16)
    to_far[...] = choose(flags, right, left).astype(BF16)


def finish_kernel(flags, total, from_far, from_near, raised, out, rows_ref):
    lane = lanes((96, 128))
    edge = (lane < 48) | (lane >= 80)
    near, far = from_near[...].astype(F32), from_far[...].astype(F32)
    left, right = choose(flags, near, far), choose(flags, far, near)
    for part in range(2):
        rows = slice(part * 96, part * 96 + 96)
        from_l = roll_lanes(left, 24 - 64 * part)
        from_r = roll_lanes(right, 80 - 64 * part)
        use_l = (lane >= 24) & (lane < 48)
        use_r = (lane >= 80) & (lane < 104)
        summed = total[rows, :] + jnp.where(use_l, from_l, jnp.where(use_r, from_r, 0.0))
        blended = summed * jnp.where(edge, 0.5, 1.0)
        value = raised[96 + part * 96 : 192 + part * 96, :]
        value = value + (level_final - level_raised) / level_raised * (value - blended)
        rows_ref[rows, :] = roll_lanes(value, -24)
    for e in range(4):
        out[e] = rows_ref[pl.ds(e, TILE_ROWS, stride=4), 0:TILE_COLS]


def shape(dims, dtype):
    return jax.ShapeDtypeStruct(dims, dtype)


def call(kernel, operands, outs, scratch=(), scalars=0, cost=(0, 0, 0), far=()):
    operands = [
        pltpu.with_memory_space_constraint(a, pltpu.HBM) if n in far else a for n, a in enumerate(operands)
    ]
    return pl.pallas_call(
        kernel,
        out_shape=outs,
        in_specs=[pl.BlockSpec(memory_space=pltpu.SMEM)] * scalars
        + [pl.BlockSpec(memory_space=pltpu.VMEM)] * (len(operands) - scalars),
        out_specs=[pl.BlockSpec(memory_space=pltpu.VMEM)] * len(outs),
        scratch_shapes=list(scratch),
        compiler_params=pltpu.CompilerParams(vmem_limit_bytes=40 << 20),
        cost_estimate=pl.CostEstimate(flops=cost[0], bytes_accessed=cost[1], transcendentals=cost[2]),
    )(*operands)


def body(
    coarse, row_map, row_frac, col_map, col_frac, noise_init, noise_churn,
    w_state, w_cond, w_expand, w_project, w_levels, w_final,
):
    lats, lons = lax.axis_size("lat"), lax.axis_size("lon")
    up = [(i, (i + 1) % lats) for i in range(lats)]
    down = [((i + 1) % lats, i) for i in range(lats)]
    near = [(i, i ^ 1) for i in range(lons)]
    far = [(i, (i + 2 * (i % 2) - 1) % lons) for i in range(lons)]

    def swap_rows(to_upper, to_lower):
        return lax.ppermute(to_lower, "lat", up), lax.ppermute(to_upper, "lat", down)

    def swap_cols(to_near, to_far):
        from_far = lax.ppermute(to_far, "lon", far)
        return from_far, lax.ppermute(to_near, "lon", near)

    msg = shape((192, 128), BF16)
    to_upper, to_lower, own, own_coarse = call(
        pack_rows_kernel,
        (noise_init, noise_churn, coarse.transpose(2, 1, 0)),
        [msg, msg, shape((2, 192, 128), F32), shape((96, 128), F32)],
        [pltpu.VMEM((2, 192, 128), F32)],
        far=(0, 1, 2),
    )
    from_upper, from_lower = swap_rows(to_upper, to_lower)
    mean_w = np.zeros((256, 256), np.float32)
    mean_w[:128, :128] = mean_w[128:, 128:] = 4.0 / 128.0
    constants = [jnp.asarray(c, BF16) for c in (SHIFTS, BACK, mean_w, POOL, GROW)]
    prepared = call(
        prepare_kernel,
        (
            w_state.T, w_cond.T, w_expand, w_project, w_levels, w_final, jnp.asarray(PICKS, BF16), *constants, col_map.reshape(20, 128), col_frac.reshape(20, 128),
        ),
        [
            shape((128, 256), BF16), shape((256, 256), BF16), shape((256, 256), BF16),
            shape((3, 1536, 256), BF16), shape((1152, 128), BF16), shape((48, 256), BF16),
            *[shape(c.shape, BF16) for c in constants],
            shape((20, 128), jnp.int32), shape((20, 128), F32), shape((8, 128), F32),
        ],
        [pltpu.VMEM((36, 128), F32)],
        cost=(2 * 36 * 128**3, 4 << 20, 0),
        far=range(14),
    )
    weights, constants, (col_map, col_frac, flags) = prepared[:6], prepared[6:11], prepared[11:]
    wide_msg = shape((288, 128), BF16)
    to_far, to_near, strip, coarse_strip = call(
        pack_cols_kernel,
        (flags, from_upper, from_lower, own, own_coarse),
        [wide_msg, wide_msg, shape((2, ROWS, 128), F32), shape((288, 128), F32)],
    )
    from_far, from_near = swap_cols(to_near, to_far)

    field = shape((ROWS, 128), F32)
    cost = (5 * 10**9, 8 << 20, 3 * 10**6)
    den, to_upper, to_lower, state, churn, cond_rows = call(
        first_kernel,
        (
            row_map, row_frac, flags, col_map, col_frac,
            strip, coarse_strip, from_far, from_near, *weights, *constants,
        ),
        [
            field, msg, msg, field, field,
            shape((PAIRS, 80, 128), BF16),
        ],
        [pltpu.VMEM((18, COARSE_SLOTS, 128), F32), pltpu.VMEM((18, 40, COARSE_SLOTS), F32)] + CORE_SCRATCH,
        scalars=2,
        cost=cost,
        far=(0, 1),
    )
    from_upper, from_lower = swap_rows(to_upper, to_lower)
    total, to_far, to_near = call(
        add_rows_kernel, (flags, den, from_upper, from_lower), [field, msg, msg]
    )
    from_far, from_near = swap_cols(to_near, to_far)
    short_msg = shape((96, 128), BF16)
    den, to_upper, to_lower, raised = call(
        second_kernel,
        (
            flags, total, from_far, from_near, state, churn, cond_rows,
            *weights, *constants,
        ),
        [field, short_msg, short_msg, field],
        CORE_SCRATCH,
        cost=cost,
    )
    from_upper, from_lower = swap_rows(to_upper, to_lower)
    total, to_far, to_near = call(
        add_tile_rows_kernel,
        (flags, den, from_upper, from_lower),
        [shape((192, 128), F32), short_msg, short_msg],
    )
    from_far, from_near = swap_cols(to_near, to_far)
    (final,) = call(
        finish_kernel,
        (flags, total, from_far, from_near, raised),
        [shape((4, TILE_ROWS, TILE_COLS), F32)],
        [pltpu.VMEM((192, 128), F32)],
    )
    return final


def solution(mesh):
    sharded = P(None, "lat", "lon")
    return jax.shard_map(
        body,
        mesh=mesh,
        in_specs=(sharded, P(), P(), P(), P(), sharded, sharded) + (P(),) * 6,
        out_specs=sharded,
        check_vma=False,
    )
```

```python
import math

import jax
import jax.numpy as jnp
import numpy as np
from jax import lax
from jax.experimental import pallas as pl
from jax.experimental.pallas import tpu as pltpu
from jax.sharding import PartitionSpec as P

MARGIN = 24
TILE_ROWS, TILE_COLS = 48, 80
PATCH_ROWS, PATCH_COLS = 96, 128
CH = 128
ROWS = 4 * PATCH_ROWS
PAIRS = PATCH_ROWS // 2
FIRST_BATCH, LAST_BATCH = 16, 48
LEVEL1_BATCH, COND_BATCH = 12, 48
SIDE = 16
COARSE_SLOTS = 48

sigma_data = 0.5
level_first = 4.0
level_second = 1.0
level_raised = 1.5
level_final = 0.25
epsilon = 1e-06

F32 = jnp.float32
BF16 = jnp.bfloat16


def _constants():
    place = np.arange(128)
    column = 8 * (place % 16) + place // 16
    shifts = [
        (np.arange(128)[:, None] == (column + shift - 1)[None, :]).astype(np.float32) for shift in range(3)
    ]
    shifts = np.concatenate(shifts, 1)
    back = []
    for shift in range(3):
        one = (column[:, None] == (np.arange(128) + shift - 1)[None, :]).astype(np.float32)
        back += [one, one]
    back = np.concatenate(back, 0)
    pick_in = np.zeros((2, 48, 128), np.float32)
    pick_out = np.zeros((2, 48, 128), np.float32)
    pick_cond = np.zeros((2, 80, 128), np.float32)
    for pi in range(2):
        pick_cond[pi, pi * 40 + np.arange(40), np.arange(40)] = 1.0
        for dc in range(3):
            for pp in range(4):
                for e in range(4):
                    dr = pp - pi
                    if 0 <= dr <= 2:
                        pick_in[pi, dc * 16 + pp * 4 + e, (3 * dr + dc) * 4 + e] = 1.0
                    dr = pi + 2 - pp
                    if 0 <= dr <= 2:
                        pick_out[pi, dc * 16 + pp * 4 + e, (3 * dr + dc) * 4 + e] = 1.0
    picks = np.concatenate([v.reshape(-1, 128) for v in (pick_in, pick_cond, pick_out, np.eye(128))], 0)
    pool = np.zeros((9, 6, 8, 12, 16), np.float32)
    for dr in range(3):
        for dc in range(3):
            for r in range(6):
                for c in range(8):
                    rr, cc = r + dr - 1, c + dc - 1
                    if 0 <= rr < 6 and 0 <= cc < 8:
                        pool[3 * dr + dc, r, c, 2 * rr : 2 * rr + 2, 2 * cc : 2 * cc + 2] = 0.25
    pool = pool.reshape(432, 6, 2, 16).transpose(0, 2, 1, 3).reshape(432, 192)
    grow = np.zeros((12, 16, 6, 8), np.float32)
    for r in range(12):
        for c in range(16):
            grow[r, c, r // 2, c // 2] = 1.0
    grow = grow.reshape(6, 2, 16, 48).transpose(1, 0, 2, 3).reshape(192, 48)
    return shifts, back, picks, pool, grow


SHIFTS, BACK, PICKS, POOL, GROW = _constants()


def dot_nt(a, b):
    return lax.dot_general(a, b, (((1,), (1,)), ((), ())), preferred_element_type=F32)


def dot_nn(a, b):
    return jnp.dot(a, b, preferred_element_type=F32)


def lanes(shape):
    return lax.broadcasted_iota(jnp.int32, shape, 1)


def choose(flags, first, second):
    return jnp.where(flags[2:3, :] > 0.5, first, second)


def roll_lanes(value, amount):
    amount = amount % 128
    return value if amount == 0 else pltpu.roll(value, amount, 1)


def prepare_kernel(
    w_state, w_cond, w_expand, w_project, w_levels, w_final, picks, shifts, back, mean_w, pool, grow, col_map, col_frac,
    first_w, expand_w, project_w, level_w, last_level_w, final_w,
    own_shifts, own_back, own_mean_w, own_pool, own_grow, own_col_map, own_col_frac, flags, flat_final,
):
    for source, target in (
        (shifts, own_shifts), (back, own_back), (mean_w, own_mean_w), (pool, own_pool), (grow, own_grow),
        (col_map, own_col_map), (col_frac, own_col_frac),
    ):
        target[...] = source[...]
    lat, lon = lax.axis_index("lat"), lax.axis_index("lon")
    row = lax.broadcasted_iota(jnp.int32, (8, 128), 0)
    above = jnp.where(lat > 0, 0.5, 0.0)
    below = jnp.where(lat < 7, 0.5, 0.0)
    odd = jnp.where(lon % 2 == 1, 1.0, 0.0)
    flags[...] = jnp.where(row == 0, above, jnp.where(row == 1, below, odd))
    unit = picks[352:480, :]
    for k in range(9):
        flat_final[4 * k : 4 * k + 4, :] = w_final[k].astype(F32)
    final_rows = flat_final[...].astype(BF16)
    for pi in range(2):
        part = slice(pi * 128, pi * 128 + 128)
        first_w[0:48, part] = dot_nn(picks[pi * 48 : pi * 48 + 48, 0:36], w_state[...]).astype(BF16)
        first_w[48:128, part] = dot_nn(picks[96 + pi * 80 : 176 + pi * 80, 0:40], w_cond[...]).astype(BF16)
        final_w[:, part] = dot_nn(picks[256 + pi * 48 : 304 + pi * 48, 0:36], final_rows).astype(BF16)
    zero = jnp.zeros((128, 128), BF16)
    for source, target, factor in ((w_expand, expand_w, 0.5), (w_project, project_w, 1.0)):
        block = (dot_nt(unit, source[...]) * factor).astype(BF16)
        target[0:128, 0:128] = block
        target[128:256, 128:256] = block
        target[0:128, 128:256] = zero
        target[128:256, 0:128] = zero
    for level in range(3):
        for dc in range(3):
            level_w[level, (9 + dc) * 128 : (10 + dc) * 128, 0:128] = zero
            level_w[level, dc * 128 : dc * 128 + 128, 128:256] = zero
            for dr in range(3):
                block = dot_nt(unit, w_levels[level, 3 * dr + dc]).astype(BF16)
                for pi in range(2):
                    start = (3 * (dr + pi) + dc) * 128
                    level_w[level, start : start + 128, pi * 128 : pi * 128 + 128] = block
    for k in range(9):
        last_level_w[k * 128 : k * 128 + 128, :] = dot_nt(unit, w_levels[3, k]).astype(BF16)


def pack_rows_kernel(noise_init, noise_churn, coarse, to_upper, to_lower, own, own_coarse, padded):
    for which, noise in enumerate((noise_init, noise_churn)):
        for e in range(4):
            padded[which, pl.ds(e, TILE_ROWS, stride=4), 0:TILE_COLS] = noise[e]
    own_coarse[...] = jnp.zeros((96, 128), F32)
    for k in range(10):
        own_coarse[pl.ds(k, 6, stride=16), 0:40] = coarse[k].astype(F32)
    lane = lanes((96, 128))
    placed = roll_lanes(own_coarse[...], 80)
    for which in range(2):
        own[which] = padded[which]
        for target, start in ((to_upper, 0), (to_lower, 96)):
            part = padded[which, start : start + 96, :]
            if which == 0:
                part = jnp.where(lane < 80, part, placed)
            target[which * 96 : which * 96 + 96, :] = part.astype(BF16)


def pack_cols_kernel(flags, from_upper, from_lower, own, own_coarse, to_far, to_near, strip, coarse_strip):
    lane = lanes((192, 128))
    for which in range(2):
        rows = slice(which * 96, which * 96 + 96)
        strip[which, 0:96, :] = roll_lanes(from_upper[rows, :].astype(F32), MARGIN)
        strip[which, 96:288, :] = roll_lanes(own[which], MARGIN)
        strip[which, 288:384, :] = roll_lanes(from_lower[rows, :].astype(F32), MARGIN)
    left = right = None
    for group in range(4):
        part = strip[group // 2, (group % 2) * 192 : (group % 2) * 192 + 192, :]
        for_left = roll_lanes(part, 32 * group - 24)
        for_right = roll_lanes(part, 32 * group - 80)
        inside = (lane >= 32 * group) & (lane < 32 * group + 32)
        left = for_left if group == 0 else jnp.where(inside, for_left, left)
        right = for_right if group == 0 else jnp.where(inside, for_right, right)
    to_near[0:192, :] = choose(flags, left, right).astype(BF16)
    to_far[0:192, :] = choose(flags, right, left).astype(BF16)
    narrow = lanes((96, 128))
    above = roll_lanes(from_upper[0:96, :].astype(F32), -80)
    middle = own_coarse[...]
    below = roll_lanes(from_lower[0:96, :].astype(F32), -80)
    for index, part in enumerate((above, middle, below)):
        coarse_strip[index * 96 : index * 96 + 96, :] = jnp.where(narrow < 40, part, 0.0)
    packed = jnp.where(narrow < 40, above, jnp.where(narrow < 80, roll_lanes(middle, 40), roll_lanes(below, 80)))
    to_near[192:288, :] = packed.astype(BF16)
    to_far[192:288, :] = packed.astype(BF16)


def pad_store(target, row, pooled, groups):
    rows = pooled.shape[0]
    place = lax.broadcasted_iota(jnp.int32, (SIDE, 128), 0)
    target[pl.ds(row + 1, rows), SIDE : SIDE + groups * SIDE, :] = pooled.reshape(
        rows, groups * SIDE, 128
    ).astype(BF16)
    for r in range(rows):
        before = pltpu.roll(pooled[r, groups - 1], 1, 0)
        after = pltpu.roll(pooled[r, 0], SIDE - 1, 0)
        target[row + 1 + r, 0:SIDE, :] = jnp.where(place == 0, 0.0, before).astype(BF16)
        target[row + 1 + r, SIDE + groups * SIDE : 2 * SIDE + groups * SIDE, :] = jnp.where(
            place == SIDE - 1, 0.0, after
        ).astype(BF16)


def halve(values, pairs, groups):
    summed = (values[:, 0:128] + values[:, 128:256]).reshape(pairs, groups // 2, 2, SIDE, 128)
    return 0.25 * (summed[:, :, 0] + summed[:, :, 1])


def norm_silu(values, mean_w):
    squares = dot_nn((values * values).astype(BF16), mean_w)
    half = values * lax.rsqrt(squares + 4.0 * epsilon)
    return half + half * jnp.tanh(half)


def conv_rows(source, weight, pair, pairs, groups):
    taps = [
        jnp.concatenate(
            [
                source[2 * (pair + m) + rr, dc * SIDE : dc * SIDE + groups * SIDE, :]
                for m in range(pairs)
            ],
            axis=0,
        )
        for rr in range(4)
        for dc in range(3)
    ]
    return dot_nn(jnp.concatenate(taps, axis=1), weight)


CORE_SCRATCH = [
    pltpu.VMEM((3, 400, 128), F32),
    pltpu.VMEM((PAIRS, 128, 256), BF16),
    pltpu.VMEM((50, 96, 128), BF16),
    pltpu.VMEM((26, 64, 128), BF16),
    pltpu.VMEM((14, 48, 128), BF16),
    pltpu.VMEM((24, 64, 256), F32),
    pltpu.VMEM((12, 32, 256), F32),
    pltpu.VMEM((3, 392, 128), F32),
    pltpu.VMEM((3, 400, 128), F32),
]


def denoise(state, cond_rows, weights, constants, scratch, noise_level, out):
    first_w, expand_w, project_w, level_w, last_level_w, final_w = weights
    shifts, back, mean_w, pool, grow = constants
    scaled, hidden, pooled1, pooled2, pooled3, level1, level2, taps_a, taps_b = scratch
    total_sq = noise_level * noise_level + sigma_data * sigma_data

    for shift in range(3):
        scaled[shift, 0:8, :] = jnp.zeros((8, 128), F32)
        scaled[shift, 384:400, :] = jnp.zeros((16, 128), F32)
        taps_a[shift, 384:392, :] = jnp.zeros((8, 128), F32)
        taps_b[shift, 0:8, :] = jnp.zeros((8, 128), F32)
    base = (state[...] * (1.0 / math.sqrt(total_sq))).astype(BF16)
    for shift in range(3):
        scaled[shift, 4 : 4 + ROWS, :] = dot_nn(base, shifts[:, shift * 128 : shift * 128 + 128])
    for buffer, rows in ((pooled1, 50), (pooled2, 26), (pooled3, 14)):
        blank = jnp.zeros(buffer.shape[1:], BF16)
        buffer[0] = blank
        buffer[rows - 1] = blank

    def first(c, carry):
        turned = []
        for k in range(FIRST_BATCH):
            row = pl.multiple_of(8 * FIRST_BATCH * c, 8) + 8 * k
            columns = [scaled[shift, pl.ds(row, 16), :].astype(BF16) for shift in range(3)]
            turned.append(jnp.concatenate(columns + [cond_rows[FIRST_BATCH * c + k]], axis=0).T)
        pre = dot_nn(jnp.concatenate(turned, axis=0), first_w[...])
        act = norm_silu(pre, mean_w[...])
        hidden[pl.ds(FIRST_BATCH * c, FIRST_BATCH)] = act.astype(BF16).reshape(FIRST_BATCH, 128, 256)
        summed = (act[:, 0:128] + act[:, 128:256]).reshape(FIRST_BATCH, 4, 2, SIDE, 128)
        pad_store(pooled1, FIRST_BATCH * c, 0.25 * (summed[:, :, 0] + summed[:, :, 1]), 4)
        return carry

    lax.fori_loop(0, PAIRS // FIRST_BATCH, first, 0, unroll=True)

    def one(c, carry):
        act = norm_silu(conv_rows(pooled1, level_w[0], LEVEL1_BATCH * c, LEVEL1_BATCH, 4), mean_w[...])
        level1[pl.ds(LEVEL1_BATCH * c, LEVEL1_BATCH)] = act.reshape(LEVEL1_BATCH, 64, 256)
        pad_store(pooled2, LEVEL1_BATCH * c, halve(act, LEVEL1_BATCH, 4), 2)
        return carry

    lax.fori_loop(0, 24 // LEVEL1_BATCH, one, 0, unroll=True)

    act = norm_silu(conv_rows(pooled2, level_w[1], 0, 12, 2), mean_w[...])
    level2[...] = act.reshape(12, 32, 256)
    pad_store(pooled3, 0, halve(act, 12, 2), 1)

    act3 = norm_silu(conv_rows(pooled3, level_w[2], 0, 6, 1), mean_w[...])
    act3 = jnp.concatenate([act3[:, 0:128], act3[:, 128:256]], axis=0)
    shifted = dot_nn(pool[...], act3.astype(BF16)).astype(BF16)
    act4 = norm_silu(
        dot_nn(jnp.concatenate([shifted[48 * k : 48 * k + 48] for k in range(9)], axis=1), last_level_w[...]),
        mean_w[0:128, 0:128],
    )
    merged3 = act3 + dot_nn(grow[...], act4.astype(BF16))
    for a in range(12):
        start = a % 2 * 96 + a // 2 * SIDE
        above = merged3[start : start + SIDE]
        above = jnp.concatenate([above, above], axis=0)
        level2[a] = level2[a] + jnp.concatenate([above, above], axis=1)

    def last(c, carry):
        merged = []
        for k in range(LAST_BATCH):
            half_of = slice(k % 2 * 128, k % 2 * 128 + 128)
            quarter_of = slice(k // 2 % 2 * 128, k // 2 % 2 * 128 + 128)
            coarse2 = level2[LAST_BATCH // 4 * c + k // 4, :, quarter_of].reshape(2, 1, SIDE, 128)
            merged1 = level1[LAST_BATCH // 2 * c + k // 2, :, half_of].reshape(2, 2, SIDE, 128) + coarse2
            merged1 = merged1.reshape(4, 1, SIDE, 128)
            merged1 = jnp.concatenate([merged1, merged1], axis=1).reshape(128, 128)
            merged.append(jnp.concatenate([merged1, merged1], axis=1))
        merged = jnp.concatenate(merged, axis=0)
        before = hidden[pl.ds(LAST_BATCH * c, LAST_BATCH)].reshape(LAST_BATCH * 128, 256)
        joined = (before.astype(F32) + merged).astype(BF16)
        half = dot_nn(joined, expand_w[...])
        inner = (half + half * jnp.tanh(half)).astype(BF16)
        mixed = (joined.astype(F32) + dot_nn(inner, project_w[...])).astype(BF16)
        for k in range(LAST_BATCH):
            taps = dot_nt(final_w[...], mixed[128 * k : 128 * k + 128])
            row = pl.multiple_of(8 * LAST_BATCH * c, 8) + 8 * k
            for shift in range(3):
                taps_a[shift, pl.ds(row, 8), :] = taps[16 * shift : 16 * shift + 8]
                taps_b[shift, pl.ds(row + 8, 8), :] = taps[16 * shift + 8 : 16 * shift + 16]
        return carry

    lax.fori_loop(0, PAIRS // LAST_BATCH, last, 0, unroll=True)

    parts = []
    for shift in range(3):
        total = taps_a[shift, 4 : 4 + ROWS, :] + taps_b[shift, 4 : 4 + ROWS, :]
        upper = total.astype(BF16)
        parts += [upper, (total - upper.astype(F32)).astype(BF16)]
    refined = dot_nn(jnp.concatenate(parts, axis=1), back[...])
    skip_scale = sigma_data * sigma_data / total_sq
    out_scale = noise_level * sigma_data / math.sqrt(total_sq)
    out[...] = skip_scale * state[...] + out_scale * refined


def inside_rows(flags):
    row = lax.broadcasted_iota(jnp.int32, (ROWS, 128), 0)
    outside = ((row < 4 * MARGIN) & (flags[0:1, :] < 0.25)) | (
        (row >= ROWS - 4 * MARGIN) & (flags[1:2, :] < 0.25)
    )
    return jnp.logical_not(outside)


def send_rows(flags, den, to_upper, to_lower, count):
    above, below = flags[0:1, :], flags[1:2, :]
    to_upper[...] = (above * den[0:count, :]).astype(BF16)
    to_lower[...] = (below * den[ROWS - count : ROWS, :]).astype(BF16)
    half = ROWS // 2
    den[0:half, :] = (1.0 - above) * den[0:half, :]
    den[half:ROWS, :] = (1.0 - below) * den[half:ROWS, :]


def first_kernel(
    row_map, row_frac, flags, col_map, col_frac, strip, coarse_strip, from_far, from_near,
    first_w, expand_w, project_w, level_w, last_level_w, final_w, shifts, back, mean_w, pool, grow,
    den, to_upper, to_lower, state, churn, cond_rows,
    window, coarse_t, *scratch,
):
    lat, lon = lax.axis_index("lat"), lax.axis_index("lon")
    lane = lanes((192, 128))
    inside = inside_rows(flags)
    near, far = from_near[...].astype(F32), from_far[...].astype(F32)
    from_left, from_right = choose(flags, near, far), choose(flags, far, near)
    for which, target in enumerate((state, churn)):
        for part in range(2):
            group = 2 * which + part
            rows = slice(part * 192, part * 192 + 192)
            left = roll_lanes(from_left[0:192, :], -32 * group)
            right = roll_lanes(from_right[0:192, :], 104 - 32 * group)
            target[rows, :] = jnp.where(lane < 24, left, jnp.where(lane < 104, strip[which, rows, :], right))
    state[...] = jnp.where(inside, level_first * state[...], 0.0)

    narrow = lanes((96, 128))
    for t, source in enumerate((from_left, None, from_right)):
        for part in range(3):
            if source is None:
                rows = coarse_strip[part * 96 : part * 96 + 96, :]
            else:
                rows = roll_lanes(source[192:288, :], -40 * part)
            for j in range(6):
                window[part * 6 + j, t * 16 : t * 16 + 16, :] = rows[j * 16 : j * 16 + 16]
    unit = jnp.where(
        lanes((40, 128)) == lax.broadcasted_iota(jnp.int32, (40, 128), 0), 1.0, 0.0
    ).astype(BF16)
    for j in range(18):
        coarse_t[j] = dot_nt(unit, window[j].astype(BF16))

    begin = lon * TILE_COLS - MARGIN
    begin = jnp.where(begin < 0, begin + 32 * TILE_COLS, begin)
    row, skip = begin // 128, begin % 128
    after = jnp.where(row == 19, 0, row + 1)
    turn = jnp.where(skip == 0, 0, 128 - skip)
    front = lanes((1, 128)) < 128 - skip

    def stretch(ref):
        return jnp.where(
            front, pltpu.roll(ref[pl.ds(row, 1), :], turn, 1), pltpu.roll(ref[pl.ds(after, 1), :], turn, 1)
        )

    offset = stretch(col_map) - (10 * lon - 10)
    offset = jnp.where(offset < 0, offset + 320, offset)
    offset = jnp.where(offset >= 320, offset - 320, offset)
    slot = lax.broadcasted_iota(jnp.int32, (COARSE_SLOTS, 128), 0)
    tile = jnp.where(slot >= 32, 2, jnp.where(slot >= 16, 1, 0))
    column = jnp.where(slot - 16 * tile < 10, slot - 6 * tile, -1)
    fraction = stretch(col_frac)
    mix = jnp.where(column == offset, 1.0 - fraction, 0.0) + jnp.where(column == offset + 1, fraction, 0.0)
    mix = dot_nn(mix.astype(BF16), shifts[:, 128:256]).astype(BF16)

    def coarse_row(p):
        y = lat * TILE_ROWS - MARGIN + p
        within = (y >= 0) & (y < 8 * TILE_ROWS)
        y = jnp.clip(y, 0, 8 * TILE_ROWS - 1)
        at = jnp.clip(row_map[y] - (lat * 6 - 6), 0, 16)
        weight = row_frac[y]
        near = jnp.where(within, 1.0 - weight, 0.0)
        far = jnp.where(within, weight, 0.0)
        return near * coarse_t[at] + far * coarse_t[at + 1]

    def interpolate(c, carry):
        rows = [coarse_row(2 * COND_BATCH * c + k) for k in range(2 * COND_BATCH)]
        fine = dot_nn(jnp.concatenate(rows, axis=0).astype(BF16), mix)
        cond_rows[pl.ds(COND_BATCH * c, COND_BATCH)] = fine.astype(BF16).reshape(COND_BATCH, 80, 128)
        return carry

    lax.fori_loop(0, PAIRS // COND_BATCH, interpolate, 0, unroll=True)

    denoise(
        state, cond_rows, (first_w, expand_w, project_w, level_w, last_level_w, final_w),
        (shifts, back, mean_w, pool, grow), scratch, level_first, den,
    )
    send_rows(flags, den, to_upper, to_lower, 192)


def add_rows_kernel(flags, den, from_upper, from_lower, total, to_far, to_near):
    top = den[0:192, :] + from_upper[...].astype(F32)
    bottom = den[192:384, :] + from_lower[...].astype(F32)
    total[0:192, :] = top
    total[192:384, :] = bottom
    lane = lanes((192, 128))
    left = jnp.where(lane < 64, top, roll_lanes(bottom, 64))
    right = jnp.where(lane < 64, roll_lanes(top, -80), roll_lanes(bottom, 64 - 80))
    to_near[...] = choose(flags, left, right).astype(BF16)
    to_far[...] = choose(flags, right, left).astype(BF16)


def second_kernel(
    flags, total, from_far, from_near, state, churn, cond_rows,
    first_w, expand_w, project_w, level_w, last_level_w, final_w, shifts, back, mean_w, pool, grow,
    den, to_upper, to_lower, raised,
    *scratch,
):
    lane = lanes((192, 128))
    edge = (lane < 48) | (lane >= 80)
    near, far = from_near[...].astype(F32), from_far[...].astype(F32)
    left, right = choose(flags, near, far), choose(flags, far, near)
    inside = inside_rows(flags)
    for part in range(2):
        rows = slice(part * 192, part * 192 + 192)
        from_l = roll_lanes(left, -64 * part)
        from_r = roll_lanes(right, 80 - 64 * part)
        summed = total[rows, :] + jnp.where(lane < 48, from_l, jnp.where(lane >= 80, from_r, 0.0))
        blended = summed * jnp.where(edge, 0.5, 1.0)
        value = state[rows, :]
        value = value + (level_second - level_first) / level_first * (value - blended)
        value = value + math.sqrt(level_raised * level_raised - level_second * level_second) * churn[rows, :]
        raised[rows, :] = value
    raised[...] = jnp.where(inside, raised[...], 0.0)
    denoise(
        raised, cond_rows, (first_w, expand_w, project_w, level_w, last_level_w, final_w),
        (shifts, back, mean_w, pool, grow), scratch, level_raised, den,
    )
    send_rows(flags, den, to_upper, to_lower, 96)


def add_tile_rows_kernel(flags, den, from_upper, from_lower, total, to_far, to_near):
    top = den[96:192, :] + from_upper[...].astype(F32)
    bottom = den[192:288, :] + from_lower[...].astype(F32)
    total[0:96, :] = top
    total[96:192, :] = bottom
    lane = lanes((96, 128))
    left = jnp.where(lane < 64, top, roll_lanes(bottom, 64))
    right = jnp.where(lane < 64, roll_lanes(top, -104), roll_lanes(bottom, 64 - 104))
    to_near[...] = choose(flags, left, right).astype(BF16)
    to_far[...] = choose(flags, right, left).astype(BF16)


def finish_kernel(flags, total, from_far, from_near, raised, out, rows_ref):
    lane = lanes((96, 128))
    edge = (lane < 48) | (lane >= 80)
    near, far = from_near[...].astype(F32), from_far[...].astype(F32)
    left, right = choose(flags, near, far), choose(flags, far, near)
    for part in range(2):
        rows = slice(part * 96, part * 96 + 96)
        from_l = roll_lanes(left, 24 - 64 * part)
        from_r = roll_lanes(right, 80 - 64 * part)
        use_l = (lane >= 24) & (lane < 48)
        use_r = (lane >= 80) & (lane < 104)
        summed = total[rows, :] + jnp.where(use_l, from_l, jnp.where(use_r, from_r, 0.0))
        blended = summed * jnp.where(edge, 0.5, 1.0)
        value = raised[96 + part * 96 : 192 + part * 96, :]
        value = value + (level_final - level_raised) / level_raised * (value - blended)
        rows_ref[rows, :] = roll_lanes(value, -24)
    for e in range(4):
        out[e] = rows_ref[pl.ds(e, TILE_ROWS, stride=4), 0:TILE_COLS]


def shape(dims, dtype):
    return jax.ShapeDtypeStruct(dims, dtype)


def call(kernel, operands, outs, scratch=(), scalars=0, cost=(0, 0, 0), far=()):
    operands = [
        pltpu.with_memory_space_constraint(a, pltpu.HBM) if n in far else a for n, a in enumerate(operands)
    ]
    return pl.pallas_call(
        kernel,
        out_shape=outs,
        in_specs=[pl.BlockSpec(memory_space=pltpu.SMEM)] * scalars
        + [pl.BlockSpec(memory_space=pltpu.VMEM)] * (len(operands) - scalars),
        out_specs=[pl.BlockSpec(memory_space=pltpu.VMEM)] * len(outs),
        scratch_shapes=list(scratch),
        compiler_params=pltpu.CompilerParams(vmem_limit_bytes=40 << 20),
        cost_estimate=pl.CostEstimate(flops=cost[0], bytes_accessed=cost[1], transcendentals=cost[2]),
    )(*operands)


def body(
    coarse, row_map, row_frac, col_map, col_frac, noise_init, noise_churn,
    w_state, w_cond, w_expand, w_project, w_levels, w_final,
):
    lats, lons = lax.axis_size("lat"), lax.axis_size("lon")
    up = [(i, (i + 1) % lats) for i in range(lats)]
    down = [((i + 1) % lats, i) for i in range(lats)]
    near = [(i, i ^ 1) for i in range(lons)]
    far = [(i, (i + 2 * (i % 2) - 1) % lons) for i in range(lons)]

    def swap_rows(to_upper, to_lower):
        return lax.ppermute(to_lower, "lat", up), lax.ppermute(to_upper, "lat", down)

    def swap_cols(to_near, to_far):
        from_far = lax.ppermute(to_far, "lon", far)
        return from_far, lax.ppermute(to_near, "lon", near)

    msg = shape((192, 128), BF16)
    to_upper, to_lower, own, own_coarse = call(
        pack_rows_kernel,
        (noise_init, noise_churn, coarse.transpose(2, 1, 0)),
        [msg, msg, shape((2, 192, 128), F32), shape((96, 128), F32)],
        [pltpu.VMEM((2, 192, 128), F32)],
        far=(0, 1, 2),
    )
    from_upper, from_lower = swap_rows(to_upper, to_lower)
    mean_w = np.zeros((256, 256), np.float32)
    mean_w[:128, :128] = mean_w[128:, 128:] = 4.0 / 128.0
    constants = [jnp.asarray(c, BF16) for c in (SHIFTS, BACK, mean_w, POOL, GROW)]
    prepared = call(
        prepare_kernel,
        (
            w_state.T, w_cond.T, w_expand, w_project, w_levels, w_final, jnp.asarray(PICKS, BF16), *constants, col_map.reshape(20, 128), col_frac.reshape(20, 128),
        ),
        [
            shape((128, 256), BF16), shape((256, 256), BF16), shape((256, 256), BF16),
            shape((3, 1536, 256), BF16), shape((1152, 128), BF16), shape((48, 256), BF16),
            *[shape(c.shape, BF16) for c in constants],
            shape((20, 128), jnp.int32), shape((20, 128), F32), shape((8, 128), F32),
        ],
        [pltpu.VMEM((36, 128), F32)],
        cost=(2 * 36 * 128**3, 4 << 20, 0),
        far=range(14),
    )
    weights, constants, (col_map, col_frac, flags) = prepared[:6], prepared[6:11], prepared[11:]
    wide_msg = shape((288, 128), BF16)
    to_far, to_near, strip, coarse_strip = call(
        pack_cols_kernel,
        (flags, from_upper, from_lower, own, own_coarse),
        [wide_msg, wide_msg, shape((2, ROWS, 128), F32), shape((288, 128), F32)],
    )
    from_far, from_near = swap_cols(to_near, to_far)

    field = shape((ROWS, 128), F32)
    cost = (5 * 10**9, 8 << 20, 3 * 10**6)
    den, to_upper, to_lower, state, churn, cond_rows = call(
        first_kernel,
        (
            row_map, row_frac, flags, col_map, col_frac,
            strip, coarse_strip, from_far, from_near, *weights, *constants,
        ),
        [
            field, msg, msg, field, field,
            shape((PAIRS, 80, 128), BF16),
        ],
        [pltpu.VMEM((18, COARSE_SLOTS, 128), F32), pltpu.VMEM((18, 40, COARSE_SLOTS), F32)] + CORE_SCRATCH,
        scalars=2,
        cost=cost,
        far=(0, 1),
    )
    from_upper, from_lower = swap_rows(to_upper, to_lower)
    total, to_far, to_near = call(
        add_rows_kernel, (flags, den, from_upper, from_lower), [field, msg, msg]
    )
    from_far, from_near = swap_cols(to_near, to_far)
    short_msg = shape((96, 128), BF16)
    den, to_upper, to_lower, raised = call(
        second_kernel,
        (
            flags, total, from_far, from_near, state, churn, cond_rows,
            *weights, *constants,
        ),
        [field, short_msg, short_msg, field],
        CORE_SCRATCH,
        cost=cost,
    )
    from_upper, from_lower = swap_rows(to_upper, to_lower)
    total, to_far, to_near = call(
        add_tile_rows_kernel,
        (flags, den, from_upper, from_lower),
        [shape((192, 128), F32), short_msg, short_msg],
    )
    from_far, from_near = swap_cols(to_near, to_far)
    (final,) = call(
        finish_kernel,
        (flags, total, from_far, from_near, raised),
        [shape((4, TILE_ROWS, TILE_COLS), F32)],
        [pltpu.VMEM((192, 128), F32)],
    )
    return final


def solution(mesh):
    sharded = P(None, "lat", "lon")
    return jax.shard_map(
        body,
        mesh=mesh,
        in_specs=(sharded, P(), P(), P(), P(), sharded, sharded) + (P(),) * 6,
        out_specs=sharded,
        check_vma=False,
    )
```
